128 devices in a mesh: gx: 8 (over y, core), gy: 16 (over x, z).
Axes of the slice: x: 4, y: 4, z: 4, core: 2. Of those that a mesh axis runs over, the one named last changes fastest.
Arguments:
- tensor: float32 [4, 672, 128, 512], P(None, 'gx', 'gy'), may hold values from -8 to 8, as said below
- start_basis: float32 [672, 96], replicated, may hold values from -6 to 6
Outputs:
- factor: float32 [672, 96], replicated
- core_tensor: float32 [4, 96, 128, 512], P(None, None, 'gy', 'gx')
The draws below stay inside these ranges and needn't reach their ends.
Inputs may be any that keep to these rules, and one draw needn't show every extreme that they name: `tensor`: row scales and species scales vary; values stay within the bounds.
All inputs are finite; a program needn't handle non-finite values.
Results may differ from the reference program's by a relative error of at most 0.0003.
Values sent between devices are 32-bit elements; how exact they have to be, the bound alone decides.
No kernel may reach another device: no remote copies, remote signals or barrier semaphores. Data moves between devices by JAX's collectives and lax.ppermute only.
A program may use at most 128 MiB of HBM per device.

```python
import math
import jax
import jax.numpy as jnp
from jax import lax

SPECIES = 4
NX = 672
RANK = 96
POWER = 2
NY = 128
NZ = 512


def draw_tensor(key, part):
    base_key = jax.random.fold_in(key, 11)
    scale_key, species_key, noise_key = jax.random.split(base_key, 3)
    row_scale = jnp.exp(jax.random.uniform(scale_key, (1, NX, 1, 1), jnp.float32, math.log(0.3), math.log(3.0)))
    species_scale = jnp.exp(jax.random.uniform(species_key, (SPECIES, 1, 1, 1), jnp.float32, math.log(0.5), math.log(2.0)))
    noise = jnp.clip(jax.random.normal(noise_key, (SPECIES, NX, NY, NZ), jnp.float32), -4.0, 4.0)
    values = 0.3 * row_scale * species_scale * noise
    return jnp.clip(values, -8.0, 8.0)


def normal_values(rng, dims, spread, bound, kind=jnp.bfloat16):
    result = jax.random.normal(rng, dims, jnp.float32) * spread
    return jnp.minimum(jnp.maximum(result, -bound), bound).astype(kind)


def setup_inputs(seed: int = 0) -> dict:
    splits = jax.random.split(jax.random.key(seed), 3)
    tensor = draw_tensor(jax.random.fold_in(splits[2], 71), 0)
    start_basis = normal_values(splits[1], (NX, RANK), 1.0, 6.0, jnp.float32)
    return dict(tensor=tensor, start_basis=start_basis)


def reference(tensor, start_basis):

    def add_species(running, species_block):
        flattened = species_block.reshape(NX, -1)
        product = jnp.dot(flattened.astype(jnp.float32), flattened.T.astype(jnp.float32), precision=lax.Precision.HIGHEST, preferred_element_type=jnp.float32)
        return (running + product, None)
    gram, unused = lax.scan(add_species, jnp.zeros((NX, NX), jnp.float32), tensor)
    upper_factor = jnp.linalg.cholesky(gram).T
    factor = start_basis
    for iteration in range(POWER):
        inside = jnp.dot(upper_factor, factor, precision=lax.Precision.HIGHEST)
        mapped = jnp.dot(upper_factor.T, inside, precision=lax.Precision.HIGHEST)
        inner_gram = jnp.dot(mapped.T, mapped, precision=lax.Precision.HIGHEST)
        lower_factor = jnp.linalg.cholesky(inner_gram)
        factor = jax.scipy.linalg.solve_triangular(lower_factor, mapped.T, lower=True).T

    def project(species_block):
        flattened = species_block.reshape(NX, -1)
        return jnp.dot(factor.T, flattened, precision=lax.Precision.HIGHEST).reshape(RANK, NY, NZ)
    core_tensor = lax.map(project, tensor)
    return (factor, core_tensor)
```

```python
import jax
import jax.numpy as jnp
from jax import lax
from jax.experimental import pallas as pl
from jax.experimental.pallas import tpu as pltpu
from jax.sharding import PartitionSpec as P

X, R = 672, 96
ROWS = 84
TILES = 6
F32, BF16 = jnp.float32, jnp.bfloat16
NN = (((1,), (0,)), ((), ()))
NT = (((1,), (1,)), ((), ()))
VMEM_LIMIT = 56 * 1024 * 1024


def split(a):
    hi = a.astype(BF16)
    return hi, (a - hi.astype(F32)).astype(BF16)


def dot3(a, b, dims):
    d = lambda p, q: lax.dot_general(p, q, dims, preferred_element_type=F32)
    return d(a[0], b[0]) + (d(a[0], b[1]) + d(a[1], b[0]))


def dot_full(a, b, dims):
    return lax.dot_general(a, b, dims, precision=lax.Precision.HIGHEST, preferred_element_type=F32)


def perm_gx(dy, dc):
    return [(2 * y + c, 2 * ((y + dy) % 4) + (c ^ dc)) for y in range(4) for c in range(2)]


def perm_x(d):
    return [(4 * x + z, 4 * ((x + d) % 4) + z) for x in range(4) for z in range(4)]


def perm_z(d):
    return [(4 * x + z, 4 * x + (z + d) % 4) for x in range(4) for z in range(4)]


def exchange(v, axis, perm):
    got = [lax.ppermute(v, axis, perm(d)) for d in (2, 1, 3)]
    return (v + got[0]) + (got[1] + got[2])


def ring_sum(pieces):
    half = pieces[0] + lax.ppermute(pieces[1], "gx", perm_gx(0, 1))
    got = [lax.ppermute(half[d], "gx", perm_gx(d, 0)) for d in (2, 1, 3)]
    mine = (half[0] + got[0]) + (got[1] + got[2])
    mine = exchange(mine, "gy", perm_x)
    mine = exchange(mine, "gy", perm_z)
    got = {d: lax.ppermute(mine, "gx", perm_gx((4 - d) % 4, 0)) for d in (2, 1, 3)}
    full = jnp.stack([mine, got[1], got[2], got[3]])
    return jnp.stack([full, lax.ppermute(full, "gx", perm_gx(0, 1))])


def put_pieces(acc, place, out):
    y, c = place
    rows = jnp.concatenate(
        [acc[:, 128 * j : 128 * j + 128] for j in range(5)]
        + [jnp.concatenate([acc[:, 640:], jnp.zeros((R, 96), F32)], axis=1)],
        axis=0,
    )
    for cc in range(2):
        for yy in range(4):
            start = 288 * cc + 72 * yy
            out[lax.rem(c + cc, 2), lax.rem(yy - y + 4, 4)] = rows[start : start + 72]


def take_pieces(ref, place):
    y, c = place
    rows = jnp.concatenate(
        [ref[lax.rem(c + cc, 2), lax.rem(yy - y + 4, 4)] for cc in range(2) for yy in range(4)], axis=0
    )
    return jnp.concatenate([rows[96 * j : 96 * j + 96] for j in range(5)] + [rows[480:576, :32]], axis=1)


def first_kernel(pos, basis, *refs):
    blocks, (hi_out, lo_out, out), (cells, sems) = refs[:8], refs[8:11], refs[11:]
    for i in range(8):
        pltpu.make_async_copy(blocks[i], cells.at[pl.ds(pos[2 + i] * 672, 672)], sems.at[i]).start()
    f = split(basis[...])
    for i in range(8):
        pltpu.make_async_copy(blocks[i], cells.at[pl.ds(pos[2 + i] * 672, 672)], sems.at[i]).wait()
    acc = jnp.zeros((R, X), F32)
    for p in range(4):
        a = jnp.concatenate([cells[pl.ds(2 * p + q, X, stride=8), :] for q in range(2)], axis=1)
        a = split(a)
        hi_out[:, 256 * p : 256 * p + 256] = a[0]
        lo_out[:, 256 * p : 256 * p + 256] = a[1]
        z = split(dot3(f, a, NN))
        acc = acc + dot3(z, a, NT)
    put_pieces(acc, (pos[0], pos[1]), out)


def first(pos, basis_t, blocks):
    any_spec = pl.BlockSpec(memory_space=pl.ANY)
    vmem = pl.BlockSpec(memory_space=pltpu.VMEM)
    return pl.pallas_call(
        first_kernel,
        out_shape=(
            jax.ShapeDtypeStruct((X, 1024), BF16),
            jax.ShapeDtypeStruct((X, 1024), BF16),
            jax.ShapeDtypeStruct((2, 4, 72, 128), F32),
        ),
        in_specs=[pl.BlockSpec(memory_space=pltpu.SMEM), vmem] + [any_spec] * 8,
        out_specs=(vmem, vmem, vmem),
        scratch_shapes=[pltpu.VMEM((X * 8, 128), F32), pltpu.SemaphoreType.DMA((8,))],
        compiler_params=pltpu.CompilerParams(vmem_limit_bytes=VMEM_LIMIT),
        cost_estimate=pl.CostEstimate(flops=3 * 4 * X * R * 1024, bytes_accessed=6 * 2**20, transcendentals=0),
    )(pos, basis_t, *blocks)


def second_kernel(pos, m_ref, hi0, lo0, hi1, lo1, out, m_out):
    m = take_pieces(m_ref, (pos[0], pos[1]))
    m_out[...] = m
    f = split(m)
    acc = jnp.zeros((R, X), F32)
    for hi, lo in ((hi0, lo0), (hi1, lo1)):
        for p in range(4):
            a = hi[:, 256 * p : 256 * p + 256], lo[:, 256 * p : 256 * p + 256]
            z = split(dot3(f, a, NN))
            acc = acc + dot3(z, a, NT)
    put_pieces(acc, (pos[0], pos[1]), out)


def second(pos, m, fibers):
    vmem = pl.BlockSpec(memory_space=pltpu.VMEM)
    return pl.pallas_call(
        second_kernel,
        out_shape=(jax.ShapeDtypeStruct((2, 4, 72, 128), F32), jax.ShapeDtypeStruct((R, X), F32)),
        in_specs=[pl.BlockSpec(memory_space=pltpu.SMEM)] + [vmem] * 5,
        out_specs=(vmem, vmem),
        compiler_params=pltpu.CompilerParams(vmem_limit_bytes=VMEM_LIMIT),
        cost_estimate=pl.CostEstimate(flops=3 * 4 * X * R * 2048, bytes_accessed=6 * 2**20, transcendentals=0),
    )(pos, m, *fibers)


def gather_kernel(pos, w_ref, linv, out):
    out[...] = dot_full(linv[...], take_pieces(w_ref, (pos[0], pos[1])), NN)


def gathered(pos, w, linv):
    vmem = pl.BlockSpec(memory_space=pltpu.VMEM)
    return pl.pallas_call(
        gather_kernel,
        out_shape=jax.ShapeDtypeStruct((R, X), F32),
        in_specs=[pl.BlockSpec(memory_space=pltpu.SMEM), vmem, vmem],
        out_specs=vmem,
        compiler_params=pltpu.CompilerParams(vmem_limit_bytes=VMEM_LIMIT),
    )(pos, w, linv)


def core_kernel(linv, m_ref, hi0, lo0, hi1, lo1, factor_t, core):
    f = dot_full(linv[...], m_ref[...], NN)
    factor_t[...] = f
    f = split(f)
    for k, (hi, lo) in enumerate(((hi0, lo0), (hi1, lo1))):
        for y in range(8):
            a = hi[:, 128 * y : 128 * y + 128], lo[:, 128 * y : 128 * y + 128]
            core[k, y] = dot3(f, a, NN).T


def core_of(linv, m, fibers):
    vmem = pl.BlockSpec(memory_space=pltpu.VMEM)
    return pl.pallas_call(
        core_kernel,
        out_shape=(jax.ShapeDtypeStruct((R, X), F32), jax.ShapeDtypeStruct((2, 8, 128, R), F32)),
        in_specs=[vmem] * 6,
        out_specs=(vmem, vmem),
        compiler_params=pltpu.CompilerParams(vmem_limit_bytes=VMEM_LIMIT),
        cost_estimate=pl.CostEstimate(flops=3 * 2 * X * R * 2048, bytes_accessed=7 * 2**20, transcendentals=0),
    )(linv, m, *fibers)


def inverse_factor(m_t):
    inner = lax.dot_general(m_t, m_t, NT, precision=lax.Precision.HIGHEST)
    lower = jnp.linalg.cholesky(inner)
    return jax.scipy.linalg.solve_triangular(lower, jnp.eye(R, dtype=F32), lower=True)


def per_device(tensor, start_basis):
    me = lax.axis_index("gx")
    y, c = me // 2, me % 2
    offsets = [(dy, dc) for dy in (2, 1, 3, 0) for dc in (1, 0)]
    sources = [2 * ((y - dy) % 4) + (c ^ dc) for dy, dc in offsets]
    pos = jnp.stack([y, c] + sources).astype(jnp.int32)
    basis_t = start_basis.T

    fibers, total = [], None
    for k in range(2):
        blocks = []
        for dy, dc in offsets:
            block = lax.dynamic_slice(
                tensor, (2 * (c ^ dc) + k, 0, 0, 128 * ((y + dy) % 4)), (1, ROWS, 8, 128)
            ).reshape(ROWS * 8, 128)
            if dy or dc:
                block = lax.ppermute(block, "gx", perm_gx(dy, dc))
            blocks.append(block)
        hi, lo, part = first(pos, basis_t, blocks)
        fibers += [hi, lo]
        total = part if total is None else total + part

    w_part, m1 = second(pos, ring_sum(total), fibers)
    linv1 = inverse_factor(m1)
    m2 = gathered(pos, ring_sum(w_part), linv1)
    factor_t, core = core_of(inverse_factor(m2), m2, fibers)

    halves = core.reshape(2, 8, 2, 64, R)
    mine = lax.dynamic_index_in_dim(halves, c, 2, keepdims=False)
    theirs = lax.ppermute(lax.dynamic_index_in_dim(halves, 1 - c, 2, keepdims=False), "gx", perm_gx(0, 1))
    out = jnp.where(c == 0, jnp.concatenate([mine, theirs]), jnp.concatenate([theirs, mine]))
    return factor_t.T, out.transpose(0, 3, 1, 2)


def solution(mesh):
    return jax.shard_map(
        per_device,
        mesh=mesh,
        in_specs=(P(None, "gx", "gy", None), P()),
        out_specs=(P(), P(None, None, "gy", "gx")),
        check_vma=False,
    )
```

```python
import jax
import jax.numpy as jnp
from jax import lax
from jax.experimental import pallas as pl
from jax.experimental.pallas import tpu as pltpu
from jax.sharding import PartitionSpec as P

X, R = 672, 96
ROWS = 84
BLOCK = 8
HALF = 1024
F32, BF16 = jnp.float32, jnp.bfloat16
NN = (((1,), (0,)), ((), ()))
NT = (((1,), (1,)), ((), ()))
VMEM_LIMIT = 56 * 1024 * 1024
STARTS = (0, 672, 1216, 1632, 1920)


def split(a):
    hi = a.astype(BF16)
    return hi, (a - hi.astype(F32)).astype(BF16)


def dot3(a, b, dims):
    d = lambda p, q: lax.dot_general(p, q, dims, preferred_element_type=F32)
    return d(a[0], b[0]) + (d(a[0], b[1]) + d(a[1], b[0]))


def dot_full(a, b, dims):
    return lax.dot_general(a, b, dims, precision=lax.Precision.HIGHEST, preferred_element_type=F32)


def perm_gx(dy, dc):
    return [(2 * y + c, 2 * ((y + dy) % 4) + (c ^ dc)) for y in range(4) for c in range(2)]


SAME_CORE = [[(2 * y + c) * 16 + k for y in range(4) for k in range(16)] for c in range(2)]


def total_over_devices(mine, other):
    half = mine + lax.ppermute(other, "gx", perm_gx(0, 1))
    both = ("gx", "gy")
    parts = lax.all_to_all(half.reshape(64, 16, 128), both, 0, 0, axis_index_groups=SAME_CORE)
    piece = jnp.sum(parts, 0)
    whole = lax.all_to_all(
        jnp.broadcast_to(piece[None], (64, 16, 128)), both, 0, 0, axis_index_groups=SAME_CORE
    ).reshape(HALF, 128)
    return whole, lax.ppermute(whole, "gx", perm_gx(0, 1))


def gram_kernel(pos, *refs):
    n = len(refs) - 8 - 6
    blocks, before = refs[:8], refs[8 : 8 + n]
    hi, lo, mine, other, cells, sems = refs[8 + n : 8 + n + 6]
    packed = cells.at[pl.ds(0, 2 * HALF)]
    for i in range(8):
        pltpu.make_async_copy(blocks[i], cells.at[pl.ds(pos[2 + i] * 672, 672)], sems.at[i]).start()
    for i in range(8):
        pltpu.make_async_copy(blocks[i], cells.at[pl.ds(pos[2 + i] * 672, 672)], sems.at[i]).wait()
    for q in range(8):
        a = split(cells[pl.ds(q, X, stride=8), :])
        hi[:, 128 * q : 128 * q + 128] = a[0]
        lo[:, 128 * q : 128 * q + 128] = a[1]
    for j in range(3):
        low, high = 256 * j, min(256 * j + 256, X)
        g = dot3((hi[low:, :], lo[low:, :]), (hi[low:high, :], lo[low:high, :]), NT)
        for t in (2 * j, 2 * j + 1):
            col = g[128 * (t % 2) : , 128 * (t % 2) : 128 * (t % 2) + 128]
            if t < 4:
                packed[STARTS[t] : STARTS[t] + X - 128 * t, :] = col
            elif t == 4:
                packed[STARTS[4] : STARTS[4] + 128, :] = col[:128]
                packed[STARTS[1] : STARTS[1] + 32, 64:] = col[128:160, :64]
                packed[STARTS[1] + 32 : STARTS[1] + 64, 64:] = col[128:160, 64:]
            else:
                packed[0:32, 96:] = col[:32, :32]
    c = pos[1]
    for out, k, half in ((mine, 0, c), (other, 1, 1 - c)):
        value = packed[pl.ds(pl.multiple_of(half * HALF, HALF), HALF), :]
        if n:
            value = value + before[k][...]
        out[...] = value


def gram(pos, blocks, before):
    any_spec = pl.BlockSpec(memory_space=pl.ANY)
    vmem = pl.BlockSpec(memory_space=pltpu.VMEM)
    return pl.pallas_call(
        gram_kernel,
        out_shape=(
            jax.ShapeDtypeStruct((X, 1024), BF16),
            jax.ShapeDtypeStruct((X, 1024), BF16),
            jax.ShapeDtypeStruct((HALF, 128), F32),
            jax.ShapeDtypeStruct((HALF, 128), F32),
        ),
        in_specs=[pl.BlockSpec(memory_space=pltpu.SMEM)] + [any_spec] * 8 + [vmem] * len(before),
        out_specs=(vmem,) * 4,
        scratch_shapes=[pltpu.VMEM((X * 8, 128), F32), pltpu.SemaphoreType.DMA((8,))],
        compiler_params=pltpu.CompilerParams(vmem_limit_bytes=VMEM_LIMIT),
        cost_estimate=pl.CostEstimate(flops=3 * 2 * X * X * 1024, bytes_accessed=6 * 2**20, transcendentals=0),
    )(pos, *blocks, *before)


def unpack(packed, g):
    row = lax.broadcasted_iota(jnp.int32, (128, 128), 0)
    col = lax.broadcasted_iota(jnp.int32, (128, 128), 1)
    lower = row >= col
    g[640:, 640:] = jnp.zeros((32, 128), F32)
    for j in range(5):
        at = 128 * j
        block = packed[STARTS[j] : STARTS[j] + 128, :]
        g[at : at + 128, at : at + 128] = jnp.where(lower, block, block.T)
        for i in range(j + 1, 5):
            first = STARTS[j] + 128 * (i - j)
            block = packed[first : first + 128, :]
            g[128 * i : 128 * i + 128, at : at + 128] = block
            g[at : at + 128, 128 * i : 128 * i + 128] = block.T
        if j < 4:
            last = packed[STARTS[j] + 640 - at : STARTS[j] + X - at, :]
        else:
            last = jnp.concatenate(
                [packed[STARTS[1] : STARTS[1] + 32, 64:], packed[STARTS[1] + 32 : STARTS[1] + 64, 64:]], axis=1
            )
        g[640:, at : at + 128] = last
        g[at : at + 128, 640:] = jnp.concatenate([last, jnp.zeros((96, 128), F32)], axis=0).T
    block = jnp.concatenate([packed[0:32, :], jnp.zeros((96, 128), F32)], axis=0)
    block = jnp.concatenate([block[:, 96:], jnp.zeros((128, 96), F32)], axis=1)
    g[640:, 640:] = jnp.where(lower, block, block.T)[:32]


def inverse_factor(s, work, out):
    eye = (lax.broadcasted_iota(jnp.int32, (R, 128), 0) == lax.broadcasted_iota(jnp.int32, (R, 128), 1)).astype(F32)
    work[:, 128:] = eye
    work[:, :R] = s
    work[:, R:128] = jnp.zeros((R, 128 - R), F32)
    for b in range(R // BLOCK):
        at = BLOCK * b
        left = [work[at + i : at + i + 1, :128] for i in range(BLOCK)]
        right = [work[at + i : at + i + 1, 128:] for i in range(BLOCK)]
        d = {
            (i, j): jnp.broadcast_to(left[i][:, at + j : at + j + 1], (1, 128))
            for i in range(BLOCK) for j in range(i + 1)
        }
        scaled = []
        for t in range(BLOCK):
            inverse = 1.0 / d[t, t]
            scaled.append(left[t] * inverse)
            for i in range(t + 1, BLOCK):
                m = d[i, t] * inverse
                for j in range(t + 1, i + 1):
                    d[i, j] = d[i, j] - m * d[j, t]
                left[i] = left[i] - m * left[t]
                right[i] = right[i] - m * right[t]
        root = [lax.rsqrt(d[t, t]) for t in range(BLOCK)]
        root = [q * (1.5 - 0.5 * (d[t, t] * q) * q) for t, q in enumerate(root)]
        out[at : at + BLOCK, :] = jnp.concatenate([right[t] * root[t] for t in range(BLOCK)], axis=0)
        if at + BLOCK < R:
            rows = jnp.concatenate(
                [jnp.concatenate(left, axis=0), jnp.concatenate(right, axis=0)], axis=1
            )
            step = dot_full(jnp.concatenate(scaled, axis=0).T, rows, NN)
            work[at + BLOCK :, :] = work[at + BLOCK :, :] - step[at + BLOCK : R]


def finish_kernel(pos, mine, other, basis, hi0, lo0, hi1, lo1, factor_t, core, packed, g, work, linv, a, sems):
    fibers = (hi0, lo0, hi1, lo1)
    for i in range(4):
        pltpu.make_async_copy(fibers[i], a.at[i], sems.at[i]).start()
    c = pos[1]
    packed[pl.ds(pl.multiple_of(c * HALF, HALF), HALF), :] = mine[...]
    packed[pl.ds(pl.multiple_of((1 - c) * HALF, HALF), HALF), :] = other[...]
    unpack(packed, g)
    f = basis[...]
    for _ in range(2):
        m = dot_full(f, g[:, :X], NN)
        inverse_factor(dot_full(m, m, NT), work, linv)
        f = dot_full(linv[:, :R], m, NN)
    factor_t[...] = f
    f = split(f)
    for i in range(4):
        pltpu.make_async_copy(fibers[i], a.at[i], sems.at[i]).wait()
    for k in range(2):
        for y in range(8):
            part = a[2 * k, :, 128 * y : 128 * y + 128], a[2 * k + 1, :, 128 * y : 128 * y + 128]
            core[k, y] = dot3(f, part, NN).T


def finish(pos, mine, other, basis_t, fibers):
    any_spec = pl.BlockSpec(memory_space=pl.ANY)
    vmem = pl.BlockSpec(memory_space=pltpu.VMEM)
    return pl.pallas_call(
        finish_kernel,
        out_shape=(jax.ShapeDtypeStruct((R, X), F32), jax.ShapeDtypeStruct((2, 8, 128, R), F32)),
        in_specs=[pl.BlockSpec(memory_space=pltpu.SMEM)] + [vmem] * 3 + [any_spec] * 4,
        out_specs=(vmem, vmem),
        scratch_shapes=[
            pltpu.VMEM((2 * HALF, 128), F32),
            pltpu.VMEM((X, 768), F32),
            pltpu.VMEM((R, 256), F32),
            pltpu.VMEM((R, 128), F32),
            pltpu.VMEM((4, X, 1024), BF16),
            pltpu.SemaphoreType.DMA((4,)),
        ],
        compiler_params=pltpu.CompilerParams(vmem_limit_bytes=VMEM_LIMIT),
        cost_estimate=pl.CostEstimate(flops=3 * 2 * X * R * 2048, bytes_accessed=7 * 2**20, transcendentals=0),
    )(pos, mine, other, basis_t, *fibers)


def per_device(tensor, start_basis):
    me = lax.axis_index("gx")
    y, c = me // 2, me % 2
    offsets = [(dy, dc) for dy in (2, 1, 3, 0) for dc in (1, 0)]
    sources = [2 * ((y - dy) % 4) + (c ^ dc) for dy, dc in offsets]
    pos = jnp.stack([y, c] + sources).astype(jnp.int32)
    basis_t = start_basis.T

    fibers, halves = [], ()
    for k in range(2):
        blocks = []
        for dy, dc in offsets:
            block = lax.dynamic_slice(
                tensor, (2 * (c ^ dc) + k, 0, 0, 128 * ((y + dy) % 4)), (1, ROWS, 8, 128)
            ).reshape(ROWS * 8, 128)
            if dy or dc:
                block = lax.ppermute(block, "gx", perm_gx(dy, dc))
            blocks.append(block)
        hi, lo, *halves = gram(pos, blocks, halves)
        fibers += [hi, lo]

    factor_t, core = finish(pos, *total_over_devices(*halves), basis_t, fibers)

    halves = core.reshape(2, 8, 2, 64, R)
    mine = lax.dynamic_index_in_dim(halves, c, 2, keepdims=False)
    theirs = lax.ppermute(lax.dynamic_index_in_dim(halves, 1 - c, 2, keepdims=False), "gx", perm_gx(0, 1))
    out = jnp.where(c == 0, jnp.concatenate([mine, theirs]), jnp.concatenate([theirs, mine]))
    return factor_t.T, out.transpose(0, 3, 1, 2)


def solution(mesh):
    return jax.shard_map(
        per_device,
        mesh=mesh,
        in_specs=(P(None, "gx", "gy", None), P()),
        out_specs=(P(), P(None, None, "gy", "gx")),
        check_vma=False,
    )
```

```python
import jax
import jax.numpy as jnp
from jax import lax
from jax.experimental import pallas as pl
from jax.experimental.pallas import tpu as pltpu
from jax.sharding import PartitionSpec as P

X, R = 672, 96
ROWS = 84
BLOCK = 16
HALF = 1024
F32, BF16 = jnp.float32, jnp.bfloat16
NN = (((1,), (0,)), ((), ()))
NT = (((1,), (1,)), ((), ()))
VMEM_LIMIT = 56 * 1024 * 1024
STARTS = (0, 672, 1216, 1632, 1920)


def split(a):
    hi = a.astype(BF16)
    return hi, (a - hi.astype(F32)).astype(BF16)


def dot3(a, b, dims):
    d = lambda p, q: lax.dot_general(p, q, dims, preferred_element_type=F32)
    return d(a[0], b[0]) + (d(a[0], b[1]) + d(a[1], b[0]))


def dot_thin(a, b):
    def parts(v):
        first = v.astype(BF16)
        v = v - first.astype(F32)
        second = v.astype(BF16)
        return first, second, (v - second.astype(F32)).astype(BF16)

    p, q = parts(a), parts(b)
    left = jnp.concatenate([p[0], p[0], p[1], p[0], p[1], p[2]], axis=0)
    right = jnp.concatenate([q[0], q[1], q[0], q[2], q[1], q[0]], axis=0)
    return lax.dot_general(left, right, (((0,), (0,)), ((), ())), preferred_element_type=F32)


def dot_full(a, b, dims):
    return lax.dot_general(a, b, dims, precision=lax.Precision.HIGHEST, preferred_element_type=F32)


def perm_gx(dy, dc):
    return [(2 * y + c, 2 * ((y + dy) % 4) + (c ^ dc)) for y in range(4) for c in range(2)]


SAME_CORE = [[(2 * y + c) * 16 + k for y in range(4) for k in range(16)] for c in range(2)]


def total_over_devices(mine, other):
    half = mine + lax.ppermute(other, "gx", perm_gx(0, 1))
    both = ("gx", "gy")
    parts = lax.all_to_all(half.reshape(64, 16, 128), both, 0, 0, axis_index_groups=SAME_CORE)
    piece = jnp.sum(parts, 0)
    whole = lax.all_to_all(
        jnp.broadcast_to(piece[None], (64, 16, 128)), both, 0, 0, axis_index_groups=SAME_CORE
    ).reshape(HALF, 128)
    return whole, lax.ppermute(whole, "gx", perm_gx(0, 1))


def gram_kernel(pos, *refs):
    n = len(refs) - 8 - 8
    blocks, before = refs[:8], refs[8 : 8 + n]
    hi_out, lo_out, mine, other, cells, hi, lo, sems = refs[8 + n :]
    packed = cells.at[pl.ds(0, 2 * HALF)]
    for i in range(8):
        pltpu.make_async_copy(blocks[i], cells.at[pl.ds(pos[2 + i] * 672, 672)], sems.at[i]).start()
    for i in range(8):
        pltpu.make_async_copy(blocks[i], cells.at[pl.ds(pos[2 + i] * 672, 672)], sems.at[i]).wait()
    for q in range(8):
        a = split(cells[pl.ds(q, X, stride=8), :])
        hi[:, 128 * q : 128 * q + 128] = a[0]
        lo[:, 128 * q : 128 * q + 128] = a[1]
    outward = [pltpu.make_async_copy(hi, hi_out, sems.at[8]), pltpu.make_async_copy(lo, lo_out, sems.at[9])]
    for copy in outward:
        copy.start()
    for j in range(3):
        low, high = 256 * j, min(256 * j + 256, X)
        g = dot3((hi[low:, :], lo[low:, :]), (hi[low:high, :], lo[low:high, :]), NT)
        for t in (2 * j, 2 * j + 1):
            col = g[128 * (t % 2) : , 128 * (t % 2) : 128 * (t % 2) + 128]
            if t < 4:
                packed[STARTS[t] : STARTS[t] + X - 128 * t, :] = col
            elif t == 4:
                packed[STARTS[4] : STARTS[4] + 128, :] = col[:128]
                packed[STARTS[1] : STARTS[1] + 32, 64:] = col[128:160, :64]
                packed[STARTS[1] + 32 : STARTS[1] + 64, 64:] = col[128:160, 64:]
            else:
                packed[0:32, 96:] = col[:32, :32]
    c = pos[1]
    for out, k, half in ((mine, 0, c), (other, 1, 1 - c)):
        value = packed[pl.ds(pl.multiple_of(half * HALF, HALF), HALF), :]
        if n:
            value = value + before[k][...]
        out[...] = value
    for copy in outward:
        copy.wait()


def gram(pos, blocks, before):
    hbm = pl.BlockSpec(memory_space=pltpu.HBM)
    vmem = pl.BlockSpec(memory_space=pltpu.VMEM)
    return pl.pallas_call(
        gram_kernel,
        out_shape=(
            jax.ShapeDtypeStruct((X, 1024), BF16),
            jax.ShapeDtypeStruct((X, 1024), BF16),
            jax.ShapeDtypeStruct((HALF, 128), F32),
            jax.ShapeDtypeStruct((HALF, 128), F32),
        ),
        in_specs=[pl.BlockSpec(memory_space=pltpu.SMEM)] + [hbm] * 8 + [vmem] * len(before),
        out_specs=(hbm, hbm, vmem, vmem),
        scratch_shapes=[
            pltpu.VMEM((X * 8, 128), F32),
            pltpu.VMEM((X, 1024), BF16),
            pltpu.VMEM((X, 1024), BF16),
            pltpu.SemaphoreType.DMA((10,)),
        ],
        compiler_params=pltpu.CompilerParams(vmem_limit_bytes=VMEM_LIMIT),
        cost_estimate=pl.CostEstimate(flops=3 * 2 * X * X * 1024, bytes_accessed=6 * 2**20, transcendentals=0),
    )(pos, *blocks, *before)


def unpack(packed, g):
    row = lax.broadcasted_iota(jnp.int32, (128, 128), 0)
    col = lax.broadcasted_iota(jnp.int32, (128, 128), 1)
    lower = row >= col
    g[640:, 640:] = jnp.zeros((32, 128), F32)
    for j in range(5):
        at = 128 * j
        block = packed[STARTS[j] : STARTS[j] + 128, :]
        g[at : at + 128, at : at + 128] = jnp.where(lower, block, block.T)
        for i in range(j + 1, 5):
            first = STARTS[j] + 128 * (i - j)
            block = packed[first : first + 128, :]
            g[128 * i : 128 * i + 128, at : at + 128] = block
            g[at : at + 128, 128 * i : 128 * i + 128] = block.T
        if j < 4:
            last = packed[STARTS[j] + 640 - at : STARTS[j] + X - at, :]
        else:
            last = jnp.concatenate(
                [packed[STARTS[1] : STARTS[1] + 32, 64:], packed[STARTS[1] + 32 : STARTS[1] + 64, 64:]], axis=1
            )
        g[640:, at : at + 128] = last
        g[at : at + 128, 640:] = jnp.concatenate([last, jnp.zeros((96, 128), F32)], axis=0).T
    block = jnp.concatenate([packed[0:32, :], jnp.zeros((96, 128), F32)], axis=0)
    block = jnp.concatenate([block[:, 96:], jnp.zeros((128, 96), F32)], axis=1)
    g[640:, 640:] = jnp.where(lower, block, block.T)[:32]


def inverse_factor(s, work, out):
    eye = (lax.broadcasted_iota(jnp.int32, (R, 128), 0) == lax.broadcasted_iota(jnp.int32, (R, 128), 1)).astype(F32)
    work[:, 128:] = eye
    work[:, :R] = s
    work[:, R:128] = jnp.zeros((R, 128 - R), F32)
    for b in range(R // BLOCK):
        at = BLOCK * b
        left = [work[at + i : at + i + 1, :128] for i in range(BLOCK)]
        right = [work[at + i : at + i + 1, 128:] for i in range(BLOCK)]
        d = {
            (i, j): jnp.broadcast_to(left[i][:, at + j : at + j + 1], (1, 128))
            for i in range(BLOCK) for j in range(i + 1)
        }
        scaled = []
        for t in range(BLOCK):
            inverse = 1.0 / d[t, t]
            scaled.append(left[t] * inverse)
            for i in range(t + 1, BLOCK):
                m = d[i, t] * inverse
                for j in range(t + 1, i + 1):
                    d[i, j] = d[i, j] - m * d[j, t]
                left[i] = left[i] - m * left[t]
                right[i] = right[i] - m * right[t]
        root = [lax.rsqrt(d[t, t]) for t in range(BLOCK)]
        root = [q * (1.5 - 0.5 * (d[t, t] * q) * q) for t, q in enumerate(root)]
        out[at : at + BLOCK, :] = jnp.concatenate([right[t] * root[t] for t in range(BLOCK)], axis=0)
        if at + BLOCK < R:
            rows = jnp.concatenate(
                [jnp.concatenate(left, axis=0), jnp.concatenate(right, axis=0)], axis=1
            )
            step = dot_thin(jnp.concatenate(scaled, axis=0), rows)
            work[at + BLOCK :, :] = work[at + BLOCK :, :] - step[at + BLOCK : R]


def finish_kernel(pos, mine, other, basis, hi0, lo0, hi1, lo1, factor_t, core, packed, g, work, linv, a, sems):
    fibers = (hi0, lo0, hi1, lo1)
    for i in range(4):
        pltpu.make_async_copy(fibers[i], a.at[i], sems.at[i]).start()
    c = pos[1]
    packed[pl.ds(pl.multiple_of(c * HALF, HALF), HALF), :] = mine[...]
    packed[pl.ds(pl.multiple_of((1 - c) * HALF, HALF), HALF), :] = other[...]
    unpack(packed, g)
    f = basis[...]
    for _ in range(2):
        m = dot_full(f, g[:, :X], NN)
        inverse_factor(dot_full(m, m, NT), work, linv)
        f = dot_full(linv[:, :R], m, NN)
    factor_t[...] = f
    f = split(f)
    for i in range(4):
        pltpu.make_async_copy(fibers[i], a.at[i], sems.at[i]).wait()
    for k in range(2):
        for y in range(8):
            part = a[2 * k, :, 128 * y : 128 * y + 128], a[2 * k + 1, :, 128 * y : 128 * y + 128]
            value = dot3(f, part, NN).T
            core[2 * k, y] = value[:64]
            core[2 * k + 1, y] = value[64:]


def finish(pos, mine, other, basis_t, fibers):
    hbm = pl.BlockSpec(memory_space=pltpu.HBM)
    vmem = pl.BlockSpec(memory_space=pltpu.VMEM)
    return pl.pallas_call(
        finish_kernel,
        out_shape=(jax.ShapeDtypeStruct((R, X), F32), jax.ShapeDtypeStruct((4, 8, 64, R), F32)),
        in_specs=[pl.BlockSpec(memory_space=pltpu.SMEM)] + [vmem] * 3 + [hbm] * 4,
        out_specs=(vmem, vmem),
        scratch_shapes=[
            pltpu.VMEM((2 * HALF, 128), F32),
            pltpu.VMEM((X, 768), F32),
            pltpu.VMEM((R, 256), F32),
            pltpu.VMEM((R, 128), F32),
            pltpu.VMEM((4, X, 1024), BF16),
            pltpu.SemaphoreType.DMA((4,)),
        ],
        compiler_params=pltpu.CompilerParams(vmem_limit_bytes=VMEM_LIMIT),
        cost_estimate=pl.CostEstimate(flops=3 * 2 * X * R * 2048, bytes_accessed=7 * 2**20, transcendentals=0),
    )(pos, mine, other, basis_t, *fibers)


def pack_kernel(pos, species, same, across):
    rows = same.shape[0]
    a, b = species[0].reshape(rows, 128), species[1].reshape(rows, 128)
    first = lax.broadcasted_iota(jnp.int32, (rows, 128), 1) < 64
    low = jnp.where(first, a, pltpu.roll(b, 64, 1))
    high = jnp.where(first, pltpu.roll(a, 64, 1), b)
    even = pos[0] == 0
    same[...] = jnp.where(even, low, high)
    across[...] = jnp.where(even, high, low)


def pack(core_and_tile, tensor, k):
    rows = ROWS // 2
    out = pl.BlockSpec((rows * 8, 128), lambda i, pos: (i, 0))
    return pl.pallas_call(
        pack_kernel,
        grid_spec=pltpu.PrefetchScalarGridSpec(
            num_scalar_prefetch=1,
            grid=(2,),
            in_specs=[pl.BlockSpec((2, rows, 8, 128), lambda i, pos: (k, i, 0, pos[1]))],
            out_specs=(out, out),
        ),
        out_shape=(jax.ShapeDtypeStruct((ROWS * 8, 128), F32),) * 2,
        cost_estimate=pl.CostEstimate(flops=2**20, bytes_accessed=2**20, transcendentals=0),
    )(core_and_tile, tensor)


def per_device(tensor, start_basis):
    me = lax.axis_index("gx")
    y, c = me // 2, me % 2
    offsets = [(dy, dc) for dy in (1, 3, 2, 0) for dc in (1, 0)]
    sources = [2 * ((y - dy) % 4) + (c ^ dc) for dy, dc in offsets]
    pos = jnp.stack([y, c] + sources).astype(jnp.int32)
    basis_t = start_basis.T

    fibers, halves = [], ()
    for k in range(2):
        blocks = []
        for dy in (1, 3, 2, 0):
            where = jnp.stack([c, (y + dy) % 4]).astype(jnp.int32)
            if k:
                where, _ = lax.optimization_barrier((where, earlier))
            same, across = pack(where, tensor, k)
            blocks.append(lax.ppermute(across, "gx", perm_gx(dy, 1)))
            blocks.append(lax.ppermute(same, "gx", perm_gx(dy, 0)) if dy else same)
        earlier = blocks[6]
        hi, lo, *halves = gram(pos, blocks, halves)
        fibers += [hi, lo]

    factor_t, core = finish(pos, *total_over_devices(*halves), basis_t, fibers)
    return factor_t.T, core.transpose(0, 3, 1, 2)


def solution(mesh):
    return jax.shard_map(
        per_device,
        mesh=mesh,
        in_specs=(P(None, "gx", "gy", None), P()),
        out_specs=(P(), P(None, None, "gy", "gx")),
        check_vma=False,
    )
```

```python
import jax
import jax.numpy as jnp
from jax import lax
from jax.experimental import pallas as pl
from jax.experimental.pallas import tpu as pltpu
from jax.sharding import PartitionSpec as P

X, R = 672, 96
ROWS = 84
BLOCK = 16
STEPS = (0, 1, 3, 2)
HALF = 1024
F32, BF16 = jnp.float32, jnp.bfloat16
NN = (((1,), (0,)), ((), ()))
NT = (((1,), (1,)), ((), ()))
VMEM_LIMIT = 56 * 1024 * 1024
STARTS = (0, 672, 1216, 1632, 1920)


def split(a):
    hi = a.astype(BF16)
    return hi, (a - hi.astype(F32)).astype(BF16)


def dot3(a, b, dims):
    d = lambda p, q: lax.dot_general(p, q, dims, preferred_element_type=F32)
    return d(a[0], b[0]) + (d(a[0], b[1]) + d(a[1], b[0]))


def dot_thin(a, b):
    def parts(v):
        first = v.astype(BF16)
        v = v - first.astype(F32)
        second = v.astype(BF16)
        return first, second, (v - second.astype(F32)).astype(BF16)

    p, q = parts(a), parts(b)
    left = jnp.concatenate([p[0], p[0], p[1], p[0], p[1], p[2]], axis=0)
    right = jnp.concatenate([q[0], q[1], q[0], q[2], q[1], q[0]], axis=0)
    return lax.dot_general(left, right, (((0,), (0,)), ((), ())), preferred_element_type=F32)


def dot_full(a, b, dims):
    return lax.dot_general(a, b, dims, precision=lax.Precision.HIGHEST, preferred_element_type=F32)


def perm_gx(dy, dc):
    return [(2 * y + c, 2 * ((y + dy) % 4) + (c ^ dc)) for y in range(4) for c in range(2)]


SAME_CORE = [[(2 * y + c) * 16 + k for y in range(4) for k in range(16)] for c in range(2)]


def total_over_devices(mine, other):
    half = mine + lax.ppermute(other, "gx", perm_gx(0, 1))
    both = ("gx", "gy")
    parts = lax.all_to_all(half.reshape(64, 16, 128), both, 0, 0, axis_index_groups=SAME_CORE)
    piece = jnp.sum(parts, 0)
    whole = lax.all_to_all(
        jnp.broadcast_to(piece[None], (64, 16, 128)), both, 0, 0, axis_index_groups=SAME_CORE
    ).reshape(HALF, 128)
    return whole, lax.ppermute(whole, "gx", perm_gx(0, 1))


def gram_kernel(pos, *refs):
    n = len(refs) - 8 - 8
    blocks, before = refs[:8], refs[8 : 8 + n]
    hi_out, lo_out, mine, other, cells, hi, lo, sems = refs[8 + n :]
    packed = cells.at[pl.ds(0, 2 * HALF)]
    for i in range(8):
        pltpu.make_async_copy(blocks[i], cells.at[pl.ds(pos[2 + i] * 672, 672)], sems.at[i]).start()
    for i in range(8):
        pltpu.make_async_copy(blocks[i], cells.at[pl.ds(pos[2 + i] * 672, 672)], sems.at[i]).wait()
    for q in range(8):
        a = split(cells[pl.ds(q, X, stride=8), :])
        hi[:, 128 * q : 128 * q + 128] = a[0]
        lo[:, 128 * q : 128 * q + 128] = a[1]
    outward = [pltpu.make_async_copy(hi, hi_out, sems.at[8]), pltpu.make_async_copy(lo, lo_out, sems.at[9])]
    for copy in outward:
        copy.start()
    for j in range(3):
        low, high = 256 * j, min(256 * j + 256, X)
        g = dot3((hi[low:, :], lo[low:, :]), (hi[low:high, :], lo[low:high, :]), NT)
        for t in (2 * j, 2 * j + 1):
            col = g[128 * (t % 2) : , 128 * (t % 2) : 128 * (t % 2) + 128]
            if t < 4:
                packed[STARTS[t] : STARTS[t] + X - 128 * t, :] = col
            elif t == 4:
                packed[STARTS[4] : STARTS[4] + 128, :] = col[:128]
                packed[STARTS[1] : STARTS[1] + 32, 64:] = col[128:160, :64]
                packed[STARTS[1] + 32 : STARTS[1] + 64, 64:] = col[128:160, 64:]
            else:
                packed[0:32, 96:] = col[:32, :32]
    c = pos[1]
    for out, k, half in ((mine, 0, c), (other, 1, 1 - c)):
        value = packed[pl.ds(pl.multiple_of(half * HALF, HALF), HALF), :]
        if n:
            value = value + before[k][...]
        out[...] = value
    for copy in outward:
        copy.wait()


def gram(pos, blocks, before):
    hbm = pl.BlockSpec(memory_space=pltpu.HBM)
    vmem = pl.BlockSpec(memory_space=pltpu.VMEM)
    return pl.pallas_call(
        gram_kernel,
        out_shape=(
            jax.ShapeDtypeStruct((X, 1024), BF16),
            jax.ShapeDtypeStruct((X, 1024), BF16),
            jax.ShapeDtypeStruct((HALF, 128), F32),
            jax.ShapeDtypeStruct((HALF, 128), F32),
        ),
        in_specs=[pl.BlockSpec(memory_space=pltpu.SMEM)] + [hbm] * 8 + [vmem] * len(before),
        out_specs=(hbm, hbm, vmem, vmem),
        scratch_shapes=[
            pltpu.VMEM((X * 8, 128), F32),
            pltpu.VMEM((X, 1024), BF16),
            pltpu.VMEM((X, 1024), BF16),
            pltpu.SemaphoreType.DMA((10,)),
        ],
        compiler_params=pltpu.CompilerParams(vmem_limit_bytes=VMEM_LIMIT),
        cost_estimate=pl.CostEstimate(flops=3 * 2 * X * X * 1024, bytes_accessed=6 * 2**20, transcendentals=0),
    )(pos, *blocks, *before)


def unpack(packed, g):
    row = lax.broadcasted_iota(jnp.int32, (128, 128), 0)
    col = lax.broadcasted_iota(jnp.int32, (128, 128), 1)
    lower = row >= col
    g[640:, 640:] = jnp.zeros((32, 128), F32)
    for j in range(5):
        at = 128 * j
        block = packed[STARTS[j] : STARTS[j] + 128, :]
        g[at : at + 128, at : at + 128] = jnp.where(lower, block, block.T)
        for i in range(j + 1, 5):
            first = STARTS[j] + 128 * (i - j)
            block = packed[first : first + 128, :]
            g[128 * i : 128 * i + 128, at : at + 128] = block
            g[at : at + 128, 128 * i : 128 * i + 128] = block.T
        if j < 4:
            last = packed[STARTS[j] + 640 - at : STARTS[j] + X - at, :]
        else:
            last = jnp.concatenate(
                [packed[STARTS[1] : STARTS[1] + 32, 64:], packed[STARTS[1] + 32 : STARTS[1] + 64, 64:]], axis=1
            )
        g[640:, at : at + 128] = last
        g[at : at + 128, 640:] = jnp.concatenate([last, jnp.zeros((96, 128), F32)], axis=0).T
    block = jnp.concatenate([packed[0:32, :], jnp.zeros((96, 128), F32)], axis=0)
    block = jnp.concatenate([block[:, 96:], jnp.zeros((128, 96), F32)], axis=1)
    g[640:, 640:] = jnp.where(lower, block, block.T)[:32]


def inverse_factor(s, work, out):
    eye = (lax.broadcasted_iota(jnp.int32, (R, 128), 0) == lax.broadcasted_iota(jnp.int32, (R, 128), 1)).astype(F32)
    work[:, 128:] = eye
    work[:, :R] = s
    work[:, R:128] = jnp.zeros((R, 128 - R), F32)
    for b in range(R // BLOCK):
        at = BLOCK * b
        left = [work[at + i : at + i + 1, :128] for i in range(BLOCK)]
        right = [work[at + i : at + i + 1, 128:] for i in range(BLOCK)]
        d = {
            (i, j): jnp.broadcast_to(left[i][:, at + j : at + j + 1], (1, 128))
            for i in range(BLOCK) for j in range(i + 1)
        }
        scaled = []
        for t in range(BLOCK):
            inverse = 1.0 / d[t, t]
            scaled.append(left[t] * inverse)
            for i in range(t + 1, BLOCK):
                m = d[i, t] * inverse
                for j in range(t + 1, i + 1):
                    d[i, j] = d[i, j] - m * d[j, t]
                left[i] = left[i] - m * left[t]
                right[i] = right[i] - m * right[t]
        root = [lax.rsqrt(d[t, t]) for t in range(BLOCK)]
        root = [q * (1.5 - 0.5 * (d[t, t] * q) * q) for t, q in enumerate(root)]
        out[at : at + BLOCK, :] = jnp.concatenate([right[t] * root[t] for t in range(BLOCK)], axis=0)
        if at + BLOCK < R:
            rows = jnp.concatenate(
                [jnp.concatenate(left, axis=0), jnp.concatenate(right, axis=0)], axis=1
            )
            step = dot_thin(jnp.concatenate(scaled, axis=0), rows)
            work[at + BLOCK :, :] = work[at + BLOCK :, :] - step[at + BLOCK : R]


def finish_kernel(pos, mine, other, basis, hi0, lo0, hi1, lo1, factor_t, core, packed, g, work, linv, a, sems):
    fibers = (hi0, lo0, hi1, lo1)
    for i in range(4):
        pltpu.make_async_copy(fibers[i], a.at[i], sems.at[i]).start()
    c = pos[1]
    packed[pl.ds(pl.multiple_of(c * HALF, HALF), HALF), :] = mine[...]
    packed[pl.ds(pl.multiple_of((1 - c) * HALF, HALF), HALF), :] = other[...]
    unpack(packed, g)
    f = basis[...]
    for _ in range(2):
        m = dot_full(f, g[:, :X], NN)
        inverse_factor(dot_full(m, m, NT), work, linv)
        f = dot_full(linv[:, :R], m, NN)
    factor_t[...] = f
    f = split(f)
    for i in range(4):
        pltpu.make_async_copy(fibers[i], a.at[i], sems.at[i]).wait()
    for k in range(2):
        for y in range(8):
            part = a[2 * k, :, 128 * y : 128 * y + 128], a[2 * k + 1, :, 128 * y : 128 * y + 128]
            value = dot3(f, part, NN).T
            core[2 * k, y] = value[:64]
            core[2 * k + 1, y] = value[64:]


def finish(pos, mine, other, basis_t, fibers):
    hbm = pl.BlockSpec(memory_space=pltpu.HBM)
    vmem = pl.BlockSpec(memory_space=pltpu.VMEM)
    return pl.pallas_call(
        finish_kernel,
        out_shape=(jax.ShapeDtypeStruct((R, X), F32), jax.ShapeDtypeStruct((4, 8, 64, R), F32)),
        in_specs=[pl.BlockSpec(memory_space=pltpu.SMEM)] + [vmem] * 3 + [hbm] * 4,
        out_specs=(vmem, vmem),
        scratch_shapes=[
            pltpu.VMEM((2 * HALF, 128), F32),
            pltpu.VMEM((X, 768), F32),
            pltpu.VMEM((R, 256), F32),
            pltpu.VMEM((R, 128), F32),
            pltpu.VMEM((4, X, 1024), BF16),
            pltpu.SemaphoreType.DMA((4,)),
        ],
        compiler_params=pltpu.CompilerParams(vmem_limit_bytes=VMEM_LIMIT),
        cost_estimate=pl.CostEstimate(flops=3 * 2 * X * R * 2048, bytes_accessed=7 * 2**20, transcendentals=0),
    )(pos, mine, other, basis_t, *fibers)


def pack_kernel(pos, species, *outs):
    rows = outs[0].shape[0]
    first = lax.broadcasted_iota(jnp.int32, (rows, 128), 1) < 64
    even = pos[1] == 0
    for i, dy in enumerate(STEPS):
        at = pl.ds(pl.multiple_of(lax.rem(pos[0] + dy, 4) * 128, 128), 128)
        a, b = (species[q, :, :, at].reshape(rows, 128) for q in range(2))
        low = jnp.where(first, a, pltpu.roll(b, 64, 1))
        high = jnp.where(first, pltpu.roll(a, 64, 1), b)
        outs[2 * i][...] = jnp.where(even, low, high)
        outs[2 * i + 1][...] = jnp.where(even, high, low)


def pack(pos, tensor, k):
    rows = 12
    out = pl.BlockSpec((rows * 8, 128), lambda i, pos: (i, 0))
    return pl.pallas_call(
        pack_kernel,
        grid_spec=pltpu.PrefetchScalarGridSpec(
            num_scalar_prefetch=1,
            grid=(ROWS // rows,),
            in_specs=[pl.BlockSpec((2, rows, 8, 512), lambda i, pos: (k, i, 0, 0))],
            out_specs=(out,) * 8,
        ),
        out_shape=(jax.ShapeDtypeStruct((ROWS * 8, 128), F32),) * 8,
        cost_estimate=pl.CostEstimate(flops=2**20, bytes_accessed=11 * 2**19, transcendentals=0),
    )(pos, tensor)


def per_device(tensor, start_basis):
    me = lax.axis_index("gx")
    y, c = me // 2, me % 2
    sources = [2 * ((y - dy) % 4) + (c ^ dc) for dy in STEPS for dc in range(2)]
    pos = jnp.stack([y, c] + sources).astype(jnp.int32)
    basis_t = start_basis.T

    fibers, halves = [], ()
    for k in range(2):
        blocks = list(pack(pos, tensor, k))
        if k:
            for i in (3, 5):
                blocks[i], _ = lax.optimization_barrier((blocks[i], halves[0]))
        for i in range(1, 8):
            blocks[i] = lax.ppermute(blocks[i], "gx", perm_gx(STEPS[i // 2], i % 2))
        hi, lo, *halves = gram(pos, blocks, halves)
        fibers += [hi, lo]

    factor_t, core = finish(pos, *total_over_devices(*halves), basis_t, fibers)
    return factor_t.T, core.transpose(0, 3, 1, 2)


def solution(mesh):
    return jax.shard_map(
        per_device,
        mesh=mesh,
        in_specs=(P(None, "gx", "gy", None), P()),
        out_specs=(P(), P(None, None, "gy", "gx")),
        check_vma=False,
    )
```

```python
import jax
import jax.numpy as jnp
from jax import lax
from jax.experimental import pallas as pl
from jax.experimental.pallas import tpu as pltpu
from jax.sharding import PartitionSpec as P

X, R = 672, 96
ROWS = 84
BLOCK = 16
OFFSETS = ((1, 0), (3, 1), (3, 0), (0, 1), (2, 1), (2, 0), (1, 1), (0, 0))
HALF = 1024
F32, BF16 = jnp.float32, jnp.bfloat16
NN = (((1,), (0,)), ((), ()))
NT = (((1,), (1,)), ((), ()))
VMEM_LIMIT = 56 * 1024 * 1024
STARTS = (0, 672, 1216, 1632, 1920)


def split(a):
    hi = a.astype(BF16)
    return hi, (a - hi.astype(F32)).astype(BF16)


def dot3(a, b, dims):
    d = lambda p, q: lax.dot_general(p, q, dims, preferred_element_type=F32)
    return d(a[0], b[0]) + (d(a[0], b[1]) + d(a[1], b[0]))


def dot_thin(a, b):
    def parts(v):
        first = v.astype(BF16)
        v = v - first.astype(F32)
        second = v.astype(BF16)
        return first, second, (v - second.astype(F32)).astype(BF16)

    p, q = parts(a), parts(b)
    left = jnp.concatenate([p[0], p[0], p[1], p[0], p[1], p[2]], axis=0)
    right = jnp.concatenate([q[0], q[1], q[0], q[2], q[1], q[0]], axis=0)
    return lax.dot_general(left, right, (((0,), (0,)), ((), ())), preferred_element_type=F32)


def dot_full(a, b, dims):
    return lax.dot_general(a, b, dims, precision=lax.Precision.HIGHEST, preferred_element_type=F32)


def perm_gx(dy, dc):
    return [(2 * y + c, 2 * ((y + dy) % 4) + (c ^ dc)) for y in range(4) for c in range(2)]


SAME_CORE = [[(2 * y + c) * 16 + k for y in range(4) for k in range(16)] for c in range(2)]


def total_over_devices(mine, other):
    half = mine + lax.ppermute(other, "gx", perm_gx(0, 1))
    both = ("gx", "gy")
    parts = lax.all_to_all(half.reshape(64, 16, 128), both, 0, 0, axis_index_groups=SAME_CORE)
    piece = jnp.sum(parts, 0)
    whole = lax.all_to_all(
        jnp.broadcast_to(piece[None], (64, 16, 128)), both, 0, 0, axis_index_groups=SAME_CORE
    ).reshape(HALF, 128)
    return whole, lax.ppermute(whole, "gx", perm_gx(0, 1))


def place():
    me = lax.axis_index("gx")
    return lax.div(me, 2), lax.rem(me, 2)


def gathers(blocks, cells, sems):
    y, c = place()
    copies = []
    for i, (dy, dc) in enumerate(OFFSETS):
        source = 2 * lax.rem(y + 4 - dy, 4) + lax.bitwise_xor(c, dc)
        at = pl.ds(pl.multiple_of(source * 672, 672), 672)
        copies += [pltpu.make_async_copy(blocks[8 * k + i], cells.at[k, at], sems.at[k, i]) for k in range(2)]
    return copies[::2], copies[1::2]


def gram_kernel(*refs):
    blocks, (mine, other, cells, hi, lo, packed, sems) = refs[:16], refs[16:]
    copies = gathers(blocks, cells, sems)
    for k in range(2):
        for copy in copies[k]:
            copy.start()

    def put(k, start, value):
        rows = slice(start, start + value.shape[0])
        packed[rows, :] = packed[rows, :] + value if k else value

    for k in range(2):
        for copy in copies[k]:
            copy.wait()
        for q in range(8):
            at = slice(128 * q, 128 * q + 128)
            hi[k, :, at], lo[k, :, at] = split(cells[k, pl.ds(q, X, stride=8), :])
        for j in range(3):
            low, high = 256 * j, min(256 * j + 256, X)
            g = dot3((hi[k, low:, :], lo[k, low:, :]), (hi[k, low:high, :], lo[k, low:high, :]), NT)
            for t in (2 * j, 2 * j + 1):
                col = g[128 * (t % 2) :, 128 * (t % 2) : 128 * (t % 2) + 128]
                if t < 4:
                    put(k, STARTS[t], col)
                elif t == 4:
                    put(k, STARTS[4], col[:128])
                    put(k, 2 * HALF, col[128:160])
                else:
                    put(k, 2 * HALF + 32, jnp.concatenate([col, jnp.zeros((32, 96), F32)], axis=1))
    packed[STARTS[1] : STARTS[1] + 32, 64:] = packed[2 * HALF : 2 * HALF + 32, :64]
    packed[STARTS[1] + 32 : STARTS[1] + 64, 64:] = packed[2 * HALF : 2 * HALF + 32, 64:]
    packed[0:32, 96:] = packed[2 * HALF + 32 : 2 * HALF + 64, :32]
    c = place()[1]
    for out, half in ((mine, c), (other, 1 - c)):
        out[...] = packed[pl.ds(pl.multiple_of(half * HALF, HALF), HALF), :]


def gram(blocks):
    hbm = pl.BlockSpec(memory_space=pl.ANY)
    vmem = pl.BlockSpec(memory_space=pltpu.VMEM)
    return pl.pallas_call(
        gram_kernel,
        out_shape=(jax.ShapeDtypeStruct((HALF, 128), F32),) * 2,
        in_specs=[hbm] * 16,
        out_specs=(vmem, vmem),
        scratch_shapes=[
            pltpu.VMEM((2, X * 8, 128), F32),
            pltpu.VMEM((2, X, 1024), BF16),
            pltpu.VMEM((2, X, 1024), BF16),
            pltpu.VMEM((2 * HALF + 64, 128), F32),
            pltpu.SemaphoreType.DMA((2, 8)),
        ],
        compiler_params=pltpu.CompilerParams(vmem_limit_bytes=VMEM_LIMIT),
        cost_estimate=pl.CostEstimate(flops=3 * 2 * X * X * 2048, bytes_accessed=7 * 2**20, transcendentals=0),
    )(*blocks)


def unpack(packed, g):
    row = lax.broadcasted_iota(jnp.int32, (128, 128), 0)
    col = lax.broadcasted_iota(jnp.int32, (128, 128), 1)
    lower = row >= col
    g[640:, 640:] = jnp.zeros((32, 128), F32)
    for j in range(5):
        at = 128 * j
        block = packed[STARTS[j] : STARTS[j] + 128, :]
        g[at : at + 128, at : at + 128] = jnp.where(lower, block, block.T)
        for i in range(j + 1, 5):
            first = STARTS[j] + 128 * (i - j)
            block = packed[first : first + 128, :]
            g[128 * i : 128 * i + 128, at : at + 128] = block
            g[at : at + 128, 128 * i : 128 * i + 128] = block.T
        if j < 4:
            last = packed[STARTS[j] + 640 - at : STARTS[j] + X - at, :]
        else:
            last = jnp.concatenate(
                [packed[STARTS[1] : STARTS[1] + 32, 64:], packed[STARTS[1] + 32 : STARTS[1] + 64, 64:]], axis=1
            )
        g[640:, at : at + 128] = last
        g[at : at + 128, 640:] = jnp.concatenate([last, jnp.zeros((96, 128), F32)], axis=0).T
    block = jnp.concatenate([packed[0:32, :], jnp.zeros((96, 128), F32)], axis=0)
    block = jnp.concatenate([block[:, 96:], jnp.zeros((128, 96), F32)], axis=1)
    g[640:, 640:] = jnp.where(lower, block, block.T)[:32]


def inverse_factor(s, work, out):
    eye = (lax.broadcasted_iota(jnp.int32, (R, 128), 0) == lax.broadcasted_iota(jnp.int32, (R, 128), 1)).astype(F32)
    work[:, 128:] = eye
    work[:, :R] = s
    work[:, R:128] = jnp.zeros((R, 128 - R), F32)
    for b in range(R // BLOCK):
        at = BLOCK * b
        left = [work[at + i : at + i + 1, :128] for i in range(BLOCK)]
        right = [work[at + i : at + i + 1, 128:] for i in range(BLOCK)]
        d = {
            (i, j): jnp.broadcast_to(left[i][:, at + j : at + j + 1], (1, 128))
            for i in range(BLOCK) for j in range(i + 1)
        }
        scaled = []
        for t in range(BLOCK):
            inverse = 1.0 / d[t, t]
            scaled.append(left[t] * inverse)
            for i in range(t + 1, BLOCK):
                m = d[i, t] * inverse
                for j in range(t + 1, i + 1):
                    d[i, j] = d[i, j] - m * d[j, t]
                left[i] = left[i] - m * left[t]
                right[i] = right[i] - m * right[t]
        root = [lax.rsqrt(d[t, t]) for t in range(BLOCK)]
        root = [q * (1.5 - 0.5 * (d[t, t] * q) * q) for t, q in enumerate(root)]
        out[at : at + BLOCK, :] = jnp.concatenate([right[t] * root[t] for t in range(BLOCK)], axis=0)
        if at + BLOCK < R:
            rows = jnp.concatenate(
                [jnp.concatenate(left, axis=0), jnp.concatenate(right, axis=0)], axis=1
            )
            step = dot_thin(jnp.concatenate(scaled, axis=0), rows)
            work[at + BLOCK :, :] = work[at + BLOCK :, :] - step[at + BLOCK : R]


def finish_kernel(*refs):
    blocks, (mine, other, basis, factor_t, core, packed, g, work, linv, cells, sems) = refs[:16], refs[16:]
    copies = sum(gathers(blocks, cells, sems), [])
    for copy in copies:
        copy.start()
    c = place()[1]
    packed[pl.ds(pl.multiple_of(c * HALF, HALF), HALF), :] = mine[...]
    packed[pl.ds(pl.multiple_of((1 - c) * HALF, HALF), HALF), :] = other[...]
    unpack(packed, g)
    f = basis[...]
    for _ in range(2):
        m = dot_full(f, g[:, :X], NN)
        inverse_factor(dot_full(m, m, NT), work, linv)
        f = dot_full(linv[:, :R], m, NN)
    factor_t[...] = f
    f = split(f)
    for copy in copies:
        copy.wait()
    for k in range(2):
        for y in range(8):
            value = dot3(f, split(cells[k, pl.ds(y, X, stride=8), :]), NN).T
            core[2 * k, y] = value[:64]
            core[2 * k + 1, y] = value[64:]


def finish(blocks, mine, other, basis_t):
    hbm = pl.BlockSpec(memory_space=pl.ANY)
    vmem = pl.BlockSpec(memory_space=pltpu.VMEM)
    return pl.pallas_call(
        finish_kernel,
        out_shape=(jax.ShapeDtypeStruct((R, X), F32), jax.ShapeDtypeStruct((4, 8, 64, R), F32)),
        in_specs=[hbm] * 16 + [vmem] * 3,
        out_specs=(vmem, vmem),
        scratch_shapes=[
            pltpu.VMEM((2 * HALF, 128), F32),
            pltpu.VMEM((X, 768), F32),
            pltpu.VMEM((R, 256), F32),
            pltpu.VMEM((R, 128), F32),
            pltpu.VMEM((2, X * 8, 128), F32),
            pltpu.SemaphoreType.DMA((2, 8)),
        ],
        compiler_params=pltpu.CompilerParams(vmem_limit_bytes=VMEM_LIMIT),
        cost_estimate=pl.CostEstimate(flops=3 * 2 * X * R * 2048, bytes_accessed=7 * 2**20, transcendentals=0),
    )(*blocks, mine, other, basis_t)


def pack_kernel(species, *outs):
    rows = outs[0].shape[0]
    first = lax.broadcasted_iota(jnp.int32, (rows, 128), 1) < 64
    y, c = place()
    even = c == 0
    for dy in range(4):
        at = pl.ds(pl.multiple_of(lax.rem(y + dy, 4) * 128, 128), 128)
        a, b = (species[q, :, :, at].reshape(rows, 128) for q in range(2))
        low = jnp.where(first, a, pltpu.roll(b, 64, 1))
        high = jnp.where(first, pltpu.roll(a, 64, 1), b)
        outs[OFFSETS.index((dy, 0))][...] = jnp.where(even, low, high)
        outs[OFFSETS.index((dy, 1))][...] = jnp.where(even, high, low)


def pack(tensor, k):
    rows = ROWS // 2
    out = pl.BlockSpec((rows * 8, 128), lambda i: (i, 0))
    return pl.pallas_call(
        pack_kernel,
        grid=(2,),
        in_specs=[pl.BlockSpec((2, rows, 8, 512), lambda i: (k, i, 0, 0))],
        out_specs=(out,) * 8,
        out_shape=(jax.ShapeDtypeStruct((ROWS * 8, 128), F32),) * 8,
        compiler_params=pltpu.CompilerParams(vmem_limit_bytes=VMEM_LIMIT),
        cost_estimate=pl.CostEstimate(flops=2**20, bytes_accessed=11 * 2**19, transcendentals=0),
    )(tensor)


def per_device(tensor, start_basis):
    basis_t = start_basis.T
    blocks = []
    for k in range(2):
        packs = pack(tensor, k)
        blocks += [lax.ppermute(b, "gx", perm_gx(*o)) for b, o in zip(packs[:7], OFFSETS)] + [packs[7]]
    factor_t, core = finish(blocks, *total_over_devices(*gram(blocks)), basis_t)
    return factor_t.T, core.transpose(0, 3, 1, 2)


def solution(mesh):
    return jax.shard_map(
        per_device,
        mesh=mesh,
        in_specs=(P(None, "gx", "gy", None), P()),
        out_specs=(P(), P(None, None, "gy", "gx")),
        check_vma=False,
    )
```

```python
import functools

import jax
import jax.numpy as jnp
from jax import lax
from jax.experimental import pallas as pl
from jax.experimental.pallas import tpu as pltpu
from jax.sharding import PartitionSpec as P

X, R = 672, 96
ROWS = 84
BLOCK = 16
OFFSETS = ((1, 0), (3, 0), (2, 0), (1, 1), (3, 1), (2, 1), (0, 1), (0, 0))
HALF = 1024
F32, BF16 = jnp.float32, jnp.bfloat16
NN = (((1,), (0,)), ((), ()))
NT = (((1,), (1,)), ((), ()))
VMEM_LIMIT = 56 * 1024 * 1024
STARTS = (0, 672, 1216, 1632, 1920)


def split(a):
    hi = a.astype(BF16)
    return hi, (a - hi.astype(F32)).astype(BF16)


def dot3(a, b, dims):
    d = lambda p, q: lax.dot_general(p, q, dims, preferred_element_type=F32)
    return d(a[0], b[0]) + (d(a[0], b[1]) + d(a[1], b[0]))


def dot_thin(a, b):
    def parts(v):
        first = v.astype(BF16)
        v = v - first.astype(F32)
        second = v.astype(BF16)
        return first, second, (v - second.astype(F32)).astype(BF16)

    p, q = parts(a), parts(b)
    left = jnp.concatenate([p[0], p[0], p[1], p[0], p[1], p[2]], axis=0)
    right = jnp.concatenate([q[0], q[1], q[0], q[2], q[1], q[0]], axis=0)
    return lax.dot_general(left, right, (((0,), (0,)), ((), ())), preferred_element_type=F32)


def dot_full(a, b, dims):
    return lax.dot_general(a, b, dims, precision=lax.Precision.HIGHEST, preferred_element_type=F32)


def perm_gx(dy, dc):
    return [(2 * y + c, 2 * ((y + dy) % 4) + (c ^ dc)) for y in range(4) for c in range(2)]


SAME_CORE = [[(2 * y + c) * 16 + k for y in range(4) for k in range(16)] for c in range(2)]


def total_over_devices(mine, other):
    half = mine + lax.ppermute(other, "gx", perm_gx(0, 1))
    both = ("gx", "gy")
    parts = lax.all_to_all(half.reshape(64, 16, 128), both, 0, 0, axis_index_groups=SAME_CORE)
    piece = jnp.sum(parts, 0)
    whole = lax.all_to_all(
        jnp.broadcast_to(piece[None], (64, 16, 128)), both, 0, 0, axis_index_groups=SAME_CORE
    ).reshape(HALF, 128)
    return whole, lax.ppermute(whole, "gx", perm_gx(0, 1))


def place():
    me = lax.axis_index("gx")
    return lax.div(me, 2), lax.rem(me, 2)


def row_starts():
    y, c = place()
    sources = [2 * lax.rem(y + 4 - dy, 4) + lax.bitwise_xor(c, dc) for dy, dc in OFFSETS]
    return [pl.ds(pl.multiple_of(source * 672, 672), 672) for source in sources]


def gram_kernel(k, *refs):
    blocks, refs = refs[:8], refs[8:]
    if k:
        before, mine, other, cells, hi, lo, packed = refs
    else:
        packed, cells, hi, lo = refs
    for block, at in zip(blocks, row_starts()):
        cells[at, :] = block[...]

    def put(start, value):
        rows = slice(start, start + value.shape[0])
        packed[rows, :] = before[rows, :] + value if k else value

    for q in range(8):
        at = slice(128 * q, 128 * q + 128)
        hi[:, at], lo[:, at] = split(cells[pl.ds(q, X, stride=8), :])
    for j in range(3):
        low, high = 256 * j, min(256 * j + 256, X)
        g = dot3((hi[low:, :], lo[low:, :]), (hi[low:high, :], lo[low:high, :]), NT)
        for t in (2 * j, 2 * j + 1):
            col = g[128 * (t % 2) :, 128 * (t % 2) : 128 * (t % 2) + 128]
            if t < 4:
                put(STARTS[t], col)
            elif t == 4:
                put(STARTS[4], col[:128])
                put(2 * HALF, col[128:160])
            else:
                put(2 * HALF + 32, jnp.concatenate([col, jnp.zeros((32, 96), F32)], axis=1))
    if not k:
        return
    packed[STARTS[1] : STARTS[1] + 32, 64:] = packed[2 * HALF : 2 * HALF + 32, :64]
    packed[STARTS[1] + 32 : STARTS[1] + 64, 64:] = packed[2 * HALF : 2 * HALF + 32, 64:]
    packed[0:32, 96:] = packed[2 * HALF + 32 : 2 * HALF + 64, :32]
    c = place()[1]
    for out, half in ((mine, c), (other, 1 - c)):
        out[...] = packed[pl.ds(pl.multiple_of(half * HALF, HALF), HALF), :]


def gram(blocks, before):
    k = len(before)
    vmem = pl.BlockSpec(memory_space=pltpu.VMEM)
    out, half = ((2 * HALF + 64, 128), F32), jax.ShapeDtypeStruct((HALF, 128), F32)
    return pl.pallas_call(
        functools.partial(gram_kernel, k),
        out_shape=(half, half) if k else (jax.ShapeDtypeStruct(*out),),
        in_specs=[vmem] * (8 + k),
        out_specs=(vmem,) * (1 + k),
        scratch_shapes=[
            pltpu.VMEM((X * 8, 128), F32),
            pltpu.VMEM((X, 1024), BF16),
            pltpu.VMEM((X, 1024), BF16),
        ] + [pltpu.VMEM(*out)] * k,
        compiler_params=pltpu.CompilerParams(vmem_limit_bytes=VMEM_LIMIT // 2),
        cost_estimate=pl.CostEstimate(flops=3 * 2 * X * X * 1024, bytes_accessed=4 * 2**20, transcendentals=0),
    )(*blocks, *before)


def unpack(packed, g):
    row = lax.broadcasted_iota(jnp.int32, (128, 128), 0)
    col = lax.broadcasted_iota(jnp.int32, (128, 128), 1)
    lower = row >= col
    g[640:, 640:] = jnp.zeros((32, 128), F32)
    for j in range(5):
        at = 128 * j
        block = packed[STARTS[j] : STARTS[j] + 128, :]
        g[at : at + 128, at : at + 128] = jnp.where(lower, block, block.T)
        for i in range(j + 1, 5):
            first = STARTS[j] + 128 * (i - j)
            block = packed[first : first + 128, :]
            g[128 * i : 128 * i + 128, at : at + 128] = block
            g[at : at + 128, 128 * i : 128 * i + 128] = block.T
        if j < 4:
            last = packed[STARTS[j] + 640 - at : STARTS[j] + X - at, :]
        else:
            last = jnp.concatenate(
                [packed[STARTS[1] : STARTS[1] + 32, 64:], packed[STARTS[1] + 32 : STARTS[1] + 64, 64:]], axis=1
            )
        g[640:, at : at + 128] = last
        g[at : at + 128, 640:] = jnp.concatenate([last, jnp.zeros((96, 128), F32)], axis=0).T
    block = jnp.concatenate([packed[0:32, :], jnp.zeros((96, 128), F32)], axis=0)
    block = jnp.concatenate([block[:, 96:], jnp.zeros((128, 96), F32)], axis=1)
    g[640:, 640:] = jnp.where(lower, block, block.T)[:32]


def inverse_factor(s, work, out):
    eye = (lax.broadcasted_iota(jnp.int32, (R, 128), 0) == lax.broadcasted_iota(jnp.int32, (R, 128), 1)).astype(F32)
    work[:, 128:] = eye
    work[:, :R] = s
    work[:, R:128] = jnp.zeros((R, 128 - R), F32)
    for b in range(R // BLOCK):
        at = BLOCK * b
        left = [work[at + i : at + i + 1, :128] for i in range(BLOCK)]
        right = [work[at + i : at + i + 1, 128:] for i in range(BLOCK)]
        d = {
            (i, j): jnp.broadcast_to(left[i][:, at + j : at + j + 1], (1, 128))
            for i in range(BLOCK) for j in range(i + 1)
        }
        scaled = []
        for t in range(BLOCK):
            inverse = 1.0 / d[t, t]
            scaled.append(left[t] * inverse)
            for i in range(t + 1, BLOCK):
                m = d[i, t] * inverse
                for j in range(t + 1, i + 1):
                    d[i, j] = d[i, j] - m * d[j, t]
                left[i] = left[i] - m * left[t]
                right[i] = right[i] - m * right[t]
        root = [lax.rsqrt(d[t, t]) for t in range(BLOCK)]
        root = [q * (1.5 - 0.5 * (d[t, t] * q) * q) for t, q in enumerate(root)]
        out[at : at + BLOCK, :] = jnp.concatenate([right[t] * root[t] for t in range(BLOCK)], axis=0)
        if at + BLOCK < R:
            rows = jnp.concatenate(
                [jnp.concatenate(left, axis=0), jnp.concatenate(right, axis=0)], axis=1
            )
            step = dot_thin(jnp.concatenate(scaled, axis=0), rows)
            work[at + BLOCK :, :] = work[at + BLOCK :, :] - step[at + BLOCK : R]


def finish_kernel(*refs):
    blocks, (mine, other, basis, factor_t, core, packed, g, work, linv, cells, sems) = refs[:16], refs[16:]
    copies = [
        pltpu.make_async_copy(blocks[8 * k + i], cells.at[k, at], sems.at[k, i])
        for k in range(2) for i, at in enumerate(row_starts())
    ]
    for copy in copies:
        copy.start()
    c = place()[1]
    packed[pl.ds(pl.multiple_of(c * HALF, HALF), HALF), :] = mine[...]
    packed[pl.ds(pl.multiple_of((1 - c) * HALF, HALF), HALF), :] = other[...]
    unpack(packed, g)
    f = basis[...]
    for _ in range(2):
        m = dot_full(f, g[:, :X], NN)
        inverse_factor(dot_full(m, m, NT), work, linv)
        f = dot_full(linv[:, :R], m, NN)
    factor_t[...] = f
    f = split(f)
    for copy in copies:
        copy.wait()
    for k in range(2):
        for y in range(8):
            value = dot3(f, split(cells[k, pl.ds(y, X, stride=8), :]), NN).T
            core[2 * k, y] = value[:64]
            core[2 * k + 1, y] = value[64:]


def finish(blocks, mine, other, basis_t):
    hbm = pl.BlockSpec(memory_space=pl.ANY)
    vmem = pl.BlockSpec(memory_space=pltpu.VMEM)
    return pl.pallas_call(
        finish_kernel,
        out_shape=(jax.ShapeDtypeStruct((R, X), F32), jax.ShapeDtypeStruct((4, 8, 64, R), F32)),
        in_specs=[hbm] * 16 + [vmem] * 3,
        out_specs=(vmem, vmem),
        scratch_shapes=[
            pltpu.VMEM((2 * HALF, 128), F32),
            pltpu.VMEM((X, 768), F32),
            pltpu.VMEM((R, 256), F32),
            pltpu.VMEM((R, 128), F32),
            pltpu.VMEM((2, X * 8, 128), F32),
            pltpu.SemaphoreType.DMA((2, 8)),
        ],
        compiler_params=pltpu.CompilerParams(vmem_limit_bytes=VMEM_LIMIT),
        cost_estimate=pl.CostEstimate(flops=3 * 2 * X * R * 2048, bytes_accessed=7 * 2**20, transcendentals=0),
    )(*blocks, mine, other, basis_t)


def pack_kernel(species, *outs):
    rows = outs[0].shape[0]
    first = lax.broadcasted_iota(jnp.int32, (rows, 128), 1) < 64
    y, c = place()
    even = c == 0
    for dy in range(4):
        at = pl.ds(pl.multiple_of(lax.rem(y + dy, 4) * 128, 128), 128)
        a, b = (species[q, :, :, at].reshape(rows, 128) for q in range(2))
        low = jnp.where(first, a, pltpu.roll(b, 64, 1))
        high = jnp.where(first, pltpu.roll(a, 64, 1), b)
        outs[OFFSETS.index((dy, 0))][...] = jnp.where(even, low, high)
        outs[OFFSETS.index((dy, 1))][...] = jnp.where(even, high, low)


def pack(tensor, k):
    rows = ROWS // 2
    out = pl.BlockSpec((rows * 8, 128), lambda i: (i, 0))
    return pl.pallas_call(
        pack_kernel,
        grid=(2,),
        in_specs=[pl.BlockSpec((2, rows, 8, 512), lambda i: (k, i, 0, 0))],
        out_specs=(out,) * 8,
        out_shape=(jax.ShapeDtypeStruct((ROWS * 8, 128), F32),) * 8,
        compiler_params=pltpu.CompilerParams(vmem_limit_bytes=VMEM_LIMIT),
        cost_estimate=pl.CostEstimate(flops=2**20, bytes_accessed=11 * 2**19, transcendentals=0),
    )(tensor)


def per_device(tensor, start_basis):
    basis_t = start_basis.T
    blocks, grams = [], ()
    for k in range(2):
        packs = pack(tensor, k)
        part = [lax.ppermute(b, "gx", perm_gx(*o)) for b, o in zip(packs[:7], OFFSETS)] + [packs[7]]
        grams = gram(part, grams)
        blocks += part
    factor_t, core = finish(blocks, *total_over_devices(*grams), basis_t)
    return factor_t.T, core.transpose(0, 3, 1, 2)


def solution(mesh):
    return jax.shard_map(
        per_device,
        mesh=mesh,
        in_specs=(P(None, "gx", "gy", None), P()),
        out_specs=(P(), P(None, None, "gy", "gx")),
        check_vma=False,
    )
```

```python
import functools

import jax
import jax.numpy as jnp
from jax import lax
from jax.experimental import pallas as pl
from jax.experimental.pallas import tpu as pltpu
from jax.sharding import PartitionSpec as P

X, R = 672, 96
ROWS = 84
BLOCK = 16
OFFSETS = ((1, 0), (3, 0), (2, 0), (1, 1), (3, 1), (2, 1), (0, 1), (0, 0))
HALF = 1024
F32, BF16 = jnp.float32, jnp.bfloat16
NN = (((1,), (0,)), ((), ()))
NT = (((1,), (1,)), ((), ()))
VMEM_LIMIT = 56 * 1024 * 1024
STARTS = (0, 672, 1216, 1632, 1920)


def split(a):
    hi = a.astype(BF16)
    return hi, (a - hi.astype(F32)).astype(BF16)


def dot3(a, b, dims):
    d = lambda p, q: lax.dot_general(p, q, dims, preferred_element_type=F32)
    return d(a[0], b[0]) + (d(a[0], b[1]) + d(a[1], b[0]))


def dot_thin(a, b):
    def parts(v):
        first = v.astype(BF16)
        v = v - first.astype(F32)
        second = v.astype(BF16)
        return first, second, (v - second.astype(F32)).astype(BF16)

    p, q = parts(a), parts(b)
    left = jnp.concatenate([p[0], p[0], p[1], p[0], p[1], p[2]], axis=0)
    right = jnp.concatenate([q[0], q[1], q[0], q[2], q[1], q[0]], axis=0)
    return lax.dot_general(left, right, (((0,), (0,)), ((), ())), preferred_element_type=F32)


def dot_full(a, b, dims):
    return lax.dot_general(a, b, dims, precision=lax.Precision.HIGHEST, preferred_element_type=F32)


def perm_gx(dy, dc):
    return [(2 * y + c, 2 * ((y + dy) % 4) + (c ^ dc)) for y in range(4) for c in range(2)]


SAME_CORE = [[(2 * y + c) * 16 + k for y in range(4) for k in range(16)] for c in range(2)]


def total_over_devices(mine, other):
    half = mine + lax.ppermute(other, "gx", perm_gx(0, 1))
    both = ("gx", "gy")
    parts = lax.all_to_all(half.reshape(64, 16, 128), both, 0, 0, axis_index_groups=SAME_CORE)
    piece = jnp.sum(parts, 0)
    whole = lax.all_to_all(
        jnp.broadcast_to(piece[None], (64, 16, 128)), both, 0, 0, axis_index_groups=SAME_CORE
    ).reshape(HALF, 128)
    return whole, lax.ppermute(whole, "gx", perm_gx(0, 1))


def place():
    me = lax.axis_index("gx")
    return lax.div(me, 2), lax.rem(me, 2)


def row_starts():
    y, c = place()
    sources = [2 * lax.rem(y + 4 - dy, 4) + lax.bitwise_xor(c, dc) for dy, dc in OFFSETS]
    return [pl.ds(pl.multiple_of(source * 672, 672), 672) for source in sources]


def gram_kernel(k, *refs):
    blocks, refs = refs[:8], refs[8:]
    if k:
        before, mine, other, cells, hi, lo, packed = refs
    else:
        packed, cells, hi, lo = refs
    for block, at in zip(blocks, row_starts()):
        cells[at, :] = block[...]

    def put(start, value):
        rows = slice(start, start + value.shape[0])
        packed[rows, :] = before[rows, :] + value if k else value

    for q in range(8):
        at = slice(128 * q, 128 * q + 128)
        hi[:, at], lo[:, at] = split(cells[pl.ds(q, X, stride=8), :])
    for j in range(3):
        low, high = 256 * j, min(256 * j + 256, X)
        g = dot3((hi[low:, :], lo[low:, :]), (hi[low:high, :], lo[low:high, :]), NT)
        for t in (2 * j, 2 * j + 1):
            col = g[128 * (t % 2) :, 128 * (t % 2) : 128 * (t % 2) + 128]
            if t < 4:
                put(STARTS[t], col)
            elif t == 4:
                put(STARTS[4], col[:128])
                put(2 * HALF, col[128:160])
            else:
                put(2 * HALF + 32, jnp.concatenate([col, jnp.zeros((32, 96), F32)], axis=1))
    if not k:
        return
    packed[STARTS[1] : STARTS[1] + 32, 64:] = packed[2 * HALF : 2 * HALF + 32, :64]
    packed[STARTS[1] + 32 : STARTS[1] + 64, 64:] = packed[2 * HALF : 2 * HALF + 32, 64:]
    packed[0:32, 96:] = packed[2 * HALF + 32 : 2 * HALF + 64, :32]
    c = place()[1]
    for out, half in ((mine, c), (other, 1 - c)):
        out[...] = packed[pl.ds(pl.multiple_of(half * HALF, HALF), HALF), :]


def gram(blocks, before):
    k = len(before)
    vmem = pl.BlockSpec(memory_space=pltpu.VMEM)
    out, half = ((2 * HALF + 64, 128), F32), jax.ShapeDtypeStruct((HALF, 128), F32)
    return pl.pallas_call(
        functools.partial(gram_kernel, k),
        out_shape=(half, half) if k else (jax.ShapeDtypeStruct(*out),),
        in_specs=[vmem] * (8 + k),
        out_specs=(vmem,) * (1 + k),
        scratch_shapes=[
            pltpu.VMEM((X * 8, 128), F32),
            pltpu.VMEM((X, 1024), BF16),
            pltpu.VMEM((X, 1024), BF16),
        ] + [pltpu.VMEM(*out)] * k,
        compiler_params=pltpu.CompilerParams(vmem_limit_bytes=VMEM_LIMIT // 2),
        cost_estimate=pl.CostEstimate(flops=3 * 2 * X * X * 1024, bytes_accessed=4 * 2**20, transcendentals=0),
    )(*blocks, *before)


def unpack(packed, g):
    row = lax.broadcasted_iota(jnp.int32, (128, 128), 0)
    col = lax.broadcasted_iota(jnp.int32, (128, 128), 1)
    lower = row >= col
    g[640:, 640:] = jnp.zeros((32, 128), F32)
    for j in range(5):
        at = 128 * j
        block = packed[STARTS[j] : STARTS[j] + 128, :]
        g[at : at + 128, at : at + 128] = jnp.where(lower, block, block.T)
        for i in range(j + 1, 5):
            first = STARTS[j] + 128 * (i - j)
            block = packed[first : first + 128, :]
            g[128 * i : 128 * i + 128, at : at + 128] = block
            g[at : at + 128, 128 * i : 128 * i + 128] = block.T
        if j < 4:
            last = packed[STARTS[j] + 640 - at : STARTS[j] + X - at, :]
        else:
            last = jnp.concatenate(
                [packed[STARTS[1] : STARTS[1] + 32, 64:], packed[STARTS[1] + 32 : STARTS[1] + 64, 64:]], axis=1
            )
        g[640:, at : at + 128] = last
        g[at : at + 128, 640:] = jnp.concatenate([last, jnp.zeros((96, 128), F32)], axis=0).T
    block = jnp.concatenate([packed[0:32, :], jnp.zeros((96, 128), F32)], axis=0)
    block = jnp.concatenate([block[:, 96:], jnp.zeros((128, 96), F32)], axis=1)
    g[640:, 640:] = jnp.where(lower, block, block.T)[:32]


def inverse_factor(s, work, out):
    eye = (lax.broadcasted_iota(jnp.int32, (R, 128), 0) == lax.broadcasted_iota(jnp.int32, (R, 128), 1)).astype(F32)
    work[:, 128:] = eye
    work[:, :R] = s
    work[:, R:128] = jnp.zeros((R, 128 - R), F32)
    for b in range(R // BLOCK):
        at = BLOCK * b
        left = [work[at + i : at + i + 1, :128] for i in range(BLOCK)]
        right = [work[at + i : at + i + 1, 128:] for i in range(BLOCK)]
        d = {
            (i, j): jnp.broadcast_to(left[i][:, at + j : at + j + 1], (1, 128))
            for i in range(BLOCK) for j in range(i + 1)
        }
        scaled = []
        for t in range(BLOCK):
            inverse = 1.0 / d[t, t]
            scaled.append(left[t] * inverse)
            for i in range(t + 1, BLOCK):
                m = d[i, t] * inverse
                for j in range(t + 1, i + 1):
                    d[i, j] = d[i, j] - m * d[j, t]
                left[i] = left[i] - m * left[t]
                right[i] = right[i] - m * right[t]
        root = [lax.rsqrt(d[t, t]) for t in range(BLOCK)]
        root = [q * (1.5 - 0.5 * (d[t, t] * q) * q) for t, q in enumerate(root)]
        out[at : at + BLOCK, :] = jnp.concatenate([right[t] * root[t] for t in range(BLOCK)], axis=0)
        if at + BLOCK < R:
            rows = jnp.concatenate(
                [jnp.concatenate(left, axis=0), jnp.concatenate(right, axis=0)], axis=1
            )
            step = dot_thin(jnp.concatenate(scaled, axis=0), rows)
            work[at + BLOCK :, :] = work[at + BLOCK :, :] - step[at + BLOCK : R]


def finish_kernel(*refs):
    blocks, (mine, other, basis, factor_t, core, packed, g, work, linv, cells, sems) = refs[:16], refs[16:]
    copies = [
        pltpu.make_async_copy(blocks[8 * k + i], cells.at[k, at], sems.at[k, i])
        for k in range(2) for i, at in enumerate(row_starts())
    ]
    for copy in copies:
        copy.start()
    c = place()[1]
    packed[pl.ds(pl.multiple_of(c * HALF, HALF), HALF), :] = mine[...]
    packed[pl.ds(pl.multiple_of((1 - c) * HALF, HALF), HALF), :] = other[...]
    unpack(packed, g)
    f = basis[...]
    for _ in range(2):
        m = dot_full(f, g[:, :X], NN)
        inverse_factor(dot_full(m, m, NT), work, linv)
        f = dot_full(linv[:, :R], m, NN)
    factor_t[...] = f
    f = split(f)
    for copy in copies:
        copy.wait()
    for k in range(2):
        for p in range(4):
            cell = jnp.concatenate([cells[k, pl.ds(2 * p + q, X, stride=8), :] for q in range(2)], axis=1)
            value = dot3(f, split(cell), NN)
            for q in range(2):
                part = value[:, 128 * q : 128 * q + 128].T
                core[2 * k, 2 * p + q] = part[:64]
                core[2 * k + 1, 2 * p + q] = part[64:]


def finish(blocks, mine, other, basis_t):
    hbm = pl.BlockSpec(memory_space=pl.ANY)
    vmem = pl.BlockSpec(memory_space=pltpu.VMEM)
    return pl.pallas_call(
        finish_kernel,
        out_shape=(jax.ShapeDtypeStruct((R, X), F32), jax.ShapeDtypeStruct((4, 8, 64, R), F32)),
        in_specs=[hbm] * 16 + [vmem] * 3,
        out_specs=(vmem, vmem),
        scratch_shapes=[
            pltpu.VMEM((2 * HALF, 128), F32),
            pltpu.VMEM((X, 768), F32),
            pltpu.VMEM((R, 256), F32),
            pltpu.VMEM((R, 128), F32),
            pltpu.VMEM((2, X * 8, 128), F32),
            pltpu.SemaphoreType.DMA((2, 8)),
        ],
        compiler_params=pltpu.CompilerParams(vmem_limit_bytes=VMEM_LIMIT),
        cost_estimate=pl.CostEstimate(flops=3 * 2 * X * R * 2048, bytes_accessed=7 * 2**20, transcendentals=0),
    )(*blocks, mine, other, basis_t)


def pack_kernel(wanted, species, *outs):
    rows = outs[0].shape[0]
    first = lax.broadcasted_iota(jnp.int32, (rows, 128), 1) < 64
    y, c = place()
    even = c == 0
    for (dy, dc), out in zip(wanted, outs):
        at = pl.ds(pl.multiple_of(lax.rem(y + dy, 4) * 128, 128), 128)
        a, b = (species[q, :, :, at].reshape(rows, 128) for q in range(2))
        low = jnp.where(first, a, pltpu.roll(b, 64, 1))
        high = jnp.where(first, pltpu.roll(a, 64, 1), b)
        out[...] = jnp.where(even, high, low) if dc else jnp.where(even, low, high)


def pack(tensor, k, wanted):
    rows = ROWS // 2
    out = pl.BlockSpec((rows * 8, 128), lambda i: (i, 0))
    return pl.pallas_call(
        functools.partial(pack_kernel, wanted),
        grid=(2,),
        in_specs=[pl.BlockSpec((2, rows, 8, 512), lambda i: (k, i, 0, 0))],
        out_specs=(out,) * len(wanted),
        out_shape=(jax.ShapeDtypeStruct((ROWS * 8, 128), F32),) * len(wanted),
        compiler_params=pltpu.CompilerParams(vmem_limit_bytes=VMEM_LIMIT),
        cost_estimate=pl.CostEstimate(flops=2**20, bytes_accessed=11 * 2**19, transcendentals=0),
    )(tensor)


def per_device(tensor, start_basis):
    basis_t = start_basis.T
    blocks, grams = [], ()
    for k in range(2):
        cut = 0 if k else 2
        packs = list(pack(tensor, k, OFFSETS[:cut])) if cut else []
        packs += pack(tensor, k, OFFSETS[cut:])
        part = [lax.ppermute(b, "gx", perm_gx(*o)) for b, o in zip(packs[:7], OFFSETS)] + [packs[7]]
        grams = gram(part, grams)
        blocks += part
    factor_t, core = finish(blocks, *total_over_devices(*grams), basis_t)
    return factor_t.T, core.transpose(0, 3, 1, 2)


def solution(mesh):
    return jax.shard_map(
        per_device,
        mesh=mesh,
        in_specs=(P(None, "gx", "gy", None), P()),
        out_specs=(P(), P(None, None, "gy", "gx")),
        check_vma=False,
    )
```

```python
import functools

import jax
import jax.numpy as jnp
from jax import lax
from jax.experimental import pallas as pl
from jax.experimental.pallas import tpu as pltpu
from jax.sharding import PartitionSpec as P

X, R = 672, 96
ROWS = 84
BLOCK = 16
OFFSETS = ((1, 0), (3, 0), (2, 0), (1, 1), (3, 1), (2, 1), (0, 1), (0, 0))
HALF = 1024
F32, BF16 = jnp.float32, jnp.bfloat16
NN = (((1,), (0,)), ((), ()))
NT = (((1,), (1,)), ((), ()))
VMEM_LIMIT = 56 * 1024 * 1024
STARTS = (0, 672, 1216, 1632, 1920)


def split(a):
    hi = a.astype(BF16)
    return hi, (a - hi.astype(F32)).astype(BF16)


def dot3(a, b, dims):
    d = lambda p, q: lax.dot_general(p, q, dims, preferred_element_type=F32)
    return d(a[0], b[0]) + (d(a[0], b[1]) + d(a[1], b[0]))


def dot_thin(a, b):
    def parts(v):
        first = v.astype(BF16)
        v = v - first.astype(F32)
        second = v.astype(BF16)
        return first, second, (v - second.astype(F32)).astype(BF16)

    p, q = parts(a), parts(b)
    left = jnp.concatenate([p[0], p[0], p[1], p[0], p[1], p[2]], axis=0)
    right = jnp.concatenate([q[0], q[1], q[0], q[2], q[1], q[0]], axis=0)
    return lax.dot_general(left, right, (((0,), (0,)), ((), ())), preferred_element_type=F32)


def dot_full(a, b, dims):
    return lax.dot_general(a, b, dims, precision=lax.Precision.HIGHEST, preferred_element_type=F32)


def perm_gx(dy, dc):
    return [(2 * y + c, 2 * ((y + dy) % 4) + (c ^ dc)) for y in range(4) for c in range(2)]


SAME_CORE = [[(2 * y + c) * 16 + k for y in range(4) for k in range(16)] for c in range(2)]


def total_over_devices(mine, other):
    half = mine + lax.ppermute(other, "gx", perm_gx(0, 1))
    both = ("gx", "gy")
    parts = lax.all_to_all(half.reshape(64, 16, 128), both, 0, 0, axis_index_groups=SAME_CORE)
    piece = jnp.sum(parts, 0)
    whole = lax.all_to_all(
        jnp.broadcast_to(piece[None], (64, 16, 128)), both, 0, 0, axis_index_groups=SAME_CORE
    ).reshape(HALF, 128)
    return whole, lax.ppermute(whole, "gx", perm_gx(0, 1))


def place():
    me = lax.axis_index("gx")
    return lax.div(me, 2), lax.rem(me, 2)


def row_starts():
    y, c = place()
    sources = [2 * lax.rem(y + 4 - dy, 4) + lax.bitwise_xor(c, dc) for dy, dc in OFFSETS]
    return [pl.ds(pl.multiple_of(source * 672, 672), 672) for source in sources]


def gram_kernel(k, *refs):
    blocks, refs = refs[:8], refs[8:]
    if k:
        before, mine, other, cells, hi, lo, packed = refs
    else:
        packed, cells, hi, lo = refs
    for block, at in zip(blocks, row_starts()):
        cells[at, :] = block[...]

    def put(start, value):
        rows = slice(start, start + value.shape[0])
        packed[rows, :] = before[rows, :] + value if k else value

    for q in range(8):
        at = slice(128 * q, 128 * q + 128)
        hi[:, at], lo[:, at] = split(cells[pl.ds(q, X, stride=8), :])
    for j in range(3):
        low, high = 256 * j, min(256 * j + 256, X)
        g = dot3((hi[low:, :], lo[low:, :]), (hi[low:high, :], lo[low:high, :]), NT)
        for t in (2 * j, 2 * j + 1):
            col = g[128 * (t % 2) :, 128 * (t % 2) : 128 * (t % 2) + 128]
            if t < 4:
                put(STARTS[t], col)
            elif t == 4:
                put(STARTS[4], col[:128])
                put(2 * HALF, col[128:160])
            else:
                put(2 * HALF + 32, jnp.concatenate([col, jnp.zeros((32, 96), F32)], axis=1))
    if not k:
        return
    packed[STARTS[1] : STARTS[1] + 32, 64:] = packed[2 * HALF : 2 * HALF + 32, :64]
    packed[STARTS[1] + 32 : STARTS[1] + 64, 64:] = packed[2 * HALF : 2 * HALF + 32, 64:]
    packed[0:32, 96:] = packed[2 * HALF + 32 : 2 * HALF + 64, :32]
    c = place()[1]
    for out, half in ((mine, c), (other, 1 - c)):
        out[...] = packed[pl.ds(pl.multiple_of(half * HALF, HALF), HALF), :]


def gram(blocks, before):
    k = len(before)
    vmem = pl.BlockSpec(memory_space=pltpu.VMEM)
    out, half = ((2 * HALF + 64, 128), F32), jax.ShapeDtypeStruct((HALF, 128), F32)
    return pl.pallas_call(
        functools.partial(gram_kernel, k),
        out_shape=(half, half) if k else (jax.ShapeDtypeStruct(*out),),
        in_specs=[vmem] * (8 + k),
        out_specs=(vmem,) * (1 + k),
        scratch_shapes=[
            pltpu.VMEM((X * 8, 128), F32),
            pltpu.VMEM((X, 1024), BF16),
            pltpu.VMEM((X, 1024), BF16),
        ] + [pltpu.VMEM(*out)] * k,
        compiler_params=pltpu.CompilerParams(vmem_limit_bytes=VMEM_LIMIT // 2),
        cost_estimate=pl.CostEstimate(flops=3 * 2 * X * X * 1024, bytes_accessed=4 * 2**20, transcendentals=0),
    )(*blocks, *before)


def unpack(packed, g):
    row = lax.broadcasted_iota(jnp.int32, (128, 128), 0)
    col = lax.broadcasted_iota(jnp.int32, (128, 128), 1)
    lower = row >= col
    g[640:, 640:] = jnp.zeros((32, 128), F32)
    for j in range(5):
        at = 128 * j
        block = packed[STARTS[j] : STARTS[j] + 128, :]
        g[at : at + 128, at : at + 128] = jnp.where(lower, block, block.T)
        for i in range(j + 1, 5):
            first = STARTS[j] + 128 * (i - j)
            block = packed[first : first + 128, :]
            g[128 * i : 128 * i + 128, at : at + 128] = block
            g[at : at + 128, 128 * i : 128 * i + 128] = block.T
        if j < 4:
            last = packed[STARTS[j] + 640 - at : STARTS[j] + X - at, :]
        else:
            last = jnp.concatenate(
                [packed[STARTS[1] : STARTS[1] + 32, 64:], packed[STARTS[1] + 32 : STARTS[1] + 64, 64:]], axis=1
            )
        g[640:, at : at + 128] = last
        g[at : at + 128, 640:] = jnp.concatenate([last, jnp.zeros((96, 128), F32)], axis=0).T
    block = jnp.concatenate([packed[0:32, :], jnp.zeros((96, 128), F32)], axis=0)
    block = jnp.concatenate([block[:, 96:], jnp.zeros((128, 96), F32)], axis=1)
    g[640:, 640:] = jnp.where(lower, block, block.T)[:32]


def inverse_factor(s, work, out):
    eye = (lax.broadcasted_iota(jnp.int32, (R, 128), 0) == lax.broadcasted_iota(jnp.int32, (R, 128), 1)).astype(F32)
    work[:, 128:] = eye
    work[:, :R] = s
    work[:, R:128] = jnp.zeros((R, 128 - R), F32)
    for b in range(R // BLOCK):
        at = BLOCK * b
        left = [work[at + i : at + i + 1, :128] for i in range(BLOCK)]
        right = [work[at + i : at + i + 1, 128:] for i in range(BLOCK)]
        d = {
            (i, j): jnp.broadcast_to(left[i][:, at + j : at + j + 1], (1, 128))
            for i in range(BLOCK) for j in range(i + 1)
        }
        scaled = []
        for t in range(BLOCK):
            inverse = 1.0 / d[t, t]
            scaled.append(left[t] * inverse)
            for i in range(t + 1, BLOCK):
                m = d[i, t] * inverse
                for j in range(t + 1, i + 1):
                    d[i, j] = d[i, j] - m * d[j, t]
                left[i] = left[i] - m * left[t]
                right[i] = right[i] - m * right[t]
        root = [lax.rsqrt(d[t, t]) for t in range(BLOCK)]
        root = [q * (1.5 - 0.5 * (d[t, t] * q) * q) for t, q in enumerate(root)]
        out[at : at + BLOCK, :] = jnp.concatenate([right[t] * root[t] for t in range(BLOCK)], axis=0)
        if at + BLOCK < R:
            rows = jnp.concatenate(
                [jnp.concatenate(left, axis=0), jnp.concatenate(right, axis=0)], axis=1
            )
            step = dot_thin(jnp.concatenate(scaled, axis=0), rows)
            work[at + BLOCK :, :] = work[at + BLOCK :, :] - step[at + BLOCK : R]


def finish_kernel(*refs):
    blocks, (mine, other, basis, factor_t, core, packed, g, work, linv, cells, sems) = refs[:16], refs[16:]
    copies = [
        pltpu.make_async_copy(blocks[8 * k + i], cells.at[k, at], sems.at[k, i])
        for k in range(2) for i, at in enumerate(row_starts())
    ]
    for copy in copies:
        copy.start()
    c = place()[1]
    packed[pl.ds(pl.multiple_of(c * HALF, HALF), HALF), :] = mine[...]
    packed[pl.ds(pl.multiple_of((1 - c) * HALF, HALF), HALF), :] = other[...]
    unpack(packed, g)
    f = basis[...]
    for _ in range(2):
        m = dot_full(f, g[:, :X], NN)
        inverse_factor(dot_full(m, m, NT), work, linv)
        f = dot_full(linv[:, :R], m, NN)
    factor_t[...] = f
    f = split(f)
    for copy in copies:
        copy.wait()
    for k in range(2):
        for p in range(4):
            cell = jnp.concatenate([cells[k, pl.ds(2 * p + q, X, stride=8), :] for q in range(2)], axis=1)
            value = dot3(f, split(cell), NN)
            for q in range(2):
                part = value[:, 128 * q : 128 * q + 128].T
                core[2 * k, 2 * p + q] = part[:64]
                core[2 * k + 1, 2 * p + q] = part[64:]


def finish(blocks, mine, other, basis_t):
    hbm = pl.BlockSpec(memory_space=pl.ANY)
    vmem = pl.BlockSpec(memory_space=pltpu.VMEM)
    return pl.pallas_call(
        finish_kernel,
        out_shape=(jax.ShapeDtypeStruct((R, X), F32), jax.ShapeDtypeStruct((4, 8, 64, R), F32)),
        in_specs=[hbm] * 16 + [vmem] * 3,
        out_specs=(vmem, vmem),
        scratch_shapes=[
            pltpu.VMEM((2 * HALF, 128), F32),
            pltpu.VMEM((X, 768), F32),
            pltpu.VMEM((R, 256), F32),
            pltpu.VMEM((R, 128), F32),
            pltpu.VMEM((2, X * 8, 128), F32),
            pltpu.SemaphoreType.DMA((2, 8)),
        ],
        compiler_params=pltpu.CompilerParams(vmem_limit_bytes=VMEM_LIMIT),
        cost_estimate=pl.CostEstimate(flops=3 * 2 * X * R * 2048, bytes_accessed=7 * 2**20, transcendentals=0),
    )(*blocks, mine, other, basis_t)


def pack_kernel(wanted, species, *outs):
    rows = outs[0].shape[0]
    first = lax.broadcasted_iota(jnp.int32, (rows, 128), 1) < 64
    y, c = place()
    even = c == 0
    for (dy, dc), out in zip(wanted, outs):
        at = pl.ds(pl.multiple_of(lax.rem(y + dy, 4) * 128, 128), 128)
        a, b = (species[q, :, :, at].reshape(rows, 128) for q in range(2))
        low = jnp.where(first, a, pltpu.roll(b, 64, 1))
        high = jnp.where(first, pltpu.roll(a, 64, 1), b)
        out[...] = jnp.where(even, high, low) if dc else jnp.where(even, low, high)


def first_kernel(wanted, tensor, *refs):
    outs, (species, sems) = refs[:-2], refs[-2:]
    y, c = place()
    copies = []
    for i, (dy, _) in enumerate(wanted):
        at = pl.ds(pl.multiple_of(lax.rem(y + dy, 4) * 128, 128), 128)
        copies.append(pltpu.make_async_copy(tensor.at[pl.ds(0, 2), :, :, at], species.at[i], sems.at[i]))
        copies[i].start()
    rows = ROWS * 8
    first = lax.broadcasted_iota(jnp.int32, (rows, 128), 1) < 64
    for i, out in enumerate(outs):
        copies[i].wait()
        a, b = (species[i, q].reshape(rows, 128) for q in range(2))
        low = jnp.where(first, a, pltpu.roll(b, 64, 1))
        high = jnp.where(first, pltpu.roll(a, 64, 1), b)
        out[...] = jnp.where(c == 0, low, high)


def pack_first(tensor, wanted):
    n = len(wanted)
    return pl.pallas_call(
        functools.partial(first_kernel, wanted),
        in_specs=[pl.BlockSpec(memory_space=pltpu.HBM)],
        out_specs=(pl.BlockSpec(memory_space=pltpu.VMEM),) * n,
        out_shape=(jax.ShapeDtypeStruct((ROWS * 8, 128), F32),) * n,
        scratch_shapes=[pltpu.VMEM((n, 2, ROWS, 8, 128), F32), pltpu.SemaphoreType.DMA((n,))],
        compiler_params=pltpu.CompilerParams(vmem_limit_bytes=60 * 1024 * 1024),
        cost_estimate=pl.CostEstimate(flops=2**20, bytes_accessed=2**21, transcendentals=0),
    )(tensor)


def pack(tensor, k, wanted):
    rows = ROWS // 2
    out = pl.BlockSpec((rows * 8, 128), lambda i: (i, 0))
    return pl.pallas_call(
        functools.partial(pack_kernel, wanted),
        grid=(2,),
        in_specs=[pl.BlockSpec((2, rows, 8, 512), lambda i: (k, i, 0, 0))],
        out_specs=(out,) * len(wanted),
        out_shape=(jax.ShapeDtypeStruct((ROWS * 8, 128), F32),) * len(wanted),
        compiler_params=pltpu.CompilerParams(vmem_limit_bytes=VMEM_LIMIT),
        cost_estimate=pl.CostEstimate(flops=2**20, bytes_accessed=11 * 2**19, transcendentals=0),
    )(tensor)


def per_device(tensor, start_basis):
    basis_t = start_basis.T
    blocks, grams = [], ()
    for k in range(2):
        cut = 0 if k else 2
        packs = list(pack_first(tensor, OFFSETS[:cut])) if cut else []
        packs += pack(tensor, k, OFFSETS[cut:])
        part = [lax.ppermute(b, "gx", perm_gx(*o)) for b, o in zip(packs[:7], OFFSETS)] + [packs[7]]
        grams = gram(part, grams)
        blocks += part
    factor_t, core = finish(blocks, *total_over_devices(*grams), basis_t)
    return factor_t.T, core.transpose(0, 3, 1, 2)


def solution(mesh):
    return jax.shard_map(
        per_device,
        mesh=mesh,
        in_specs=(P(None, "gx", "gy", None), P()),
        out_specs=(P(), P(None, None, "gy", "gx")),
        check_vma=False,
    )
```
